32 devices in a mesh: gx: 8 (over z, x), gz: 4 (over y, core).
Axes of the slice: x: 2, y: 2, z: 4, core: 2. Of those that a mesh axis runs over, the one named last changes fastest.
Arguments:
- conserved_fields: float32 [6, 128, 128, 128], P(None, 'gx', 'gz'), may hold values from -2 to 62, as said below
- coeff: bfloat16 [2, 1024, 6, 128, 512], P(None, 'gx', None, 'gz'), may hold values from -0.25 to 0.25
- feed_plane: int32 [12], replicated, may hold values from 0 to 2047
Outputs:
- new_state: float32 [6, 128, 128, 128], P(None, 'gx', 'gz')
The draws below stay inside these ranges and needn't reach their ends.
Inputs may be any that keep to these rules, and one draw needn't show every extreme that they name: `conserved_fields`: each cell is the conserved form of a gas with density 0.5 to 2, temperature 0.5 to 2, streamwise velocity -1 to 7, wall-normal and spanwise velocities -1 to 1 and vibrational energy per unit mass 0.05 to 0.5.
All inputs are finite; a program needn't handle non-finite values.
Results may differ from the reference program's by a relative error of at most 0.00038.
Values sent between devices are 32-bit elements; how exact they have to be, the bound alone decides.
No kernel may reach another device: no remote copies, remote signals or barrier semaphores. Data moves between devices by JAX's collectives and lax.ppermute only.
A program may use at most 256 MiB of HBM per device.

```python
import math
import jax
import jax.numpy as jnp
from jax import lax

CX = 16
NY = 128
KXH = 1024
NZP = 512
NXP = 2048
NX = 128
NZ = 128
FORCE = 12
N_GX = 8


def draw_conserved_fields(key, part):
    stochastic_seeds = jax.random.split(jax.random.fold_in(key, 17), 6)
    field_extents = (NX, NZ, NY)
    fluid_rho_field = jax.random.uniform(stochastic_seeds[0], field_extents, jnp.float32, 0.5, 2.0)
    translational_kelvin = jax.random.uniform(stochastic_seeds[1], field_extents, jnp.float32, 0.5, 2.0)
    stream_vel = jax.random.uniform(stochastic_seeds[2], field_extents, jnp.float32, -1.0, 7.0)
    normal_vel = jax.random.uniform(stochastic_seeds[3], field_extents, jnp.float32, -1.0, 1.0)
    span_vel = jax.random.uniform(stochastic_seeds[4], field_extents, jnp.float32, -1.0, 1.0)
    oscillator_content = jax.random.uniform(stochastic_seeds[5], field_extents, jnp.float32, 0.05, 0.5)
    motion_share = 0.5 * (jnp.square(stream_vel) + jnp.square(normal_vel) + jnp.square(span_vel))
    overall_enthalpy_field = fluid_rho_field * (2.5 * translational_kelvin + motion_share + oscillator_content)
    return jnp.stack([fluid_rho_field, fluid_rho_field * stream_vel, fluid_rho_field * normal_vel, fluid_rho_field * span_vel, overall_enthalpy_field, fluid_rho_field * oscillator_content]).astype(jnp.float32)


def place_ends(entries, rng, low, top_value):
    longest = entries.shape.index(max(entries.shape))
    spots = []
    for shift in (0, 1):
        where = [jax.random.randint(jax.random.fold_in(rng, axis), (), 0, length) for axis, length in enumerate(entries.shape)]
        where[longest] = (where[longest] + shift) % entries.shape[longest]
        spots.append(tuple(where))
    return entries.at[spots[0]].set(low).at[spots[1]].set(top_value)


def level_of(rng, shape, cuts, least, high):
    level = 1.0
    for position, blocks in cuts:
        draws = jax.random.uniform(jax.random.fold_in(jax.random.fold_in(rng, 6), position), (blocks,), jnp.float32, least / len(cuts), high / len(cuts))
        level = level * jnp.repeat(jnp.exp(draws), shape[position] // blocks).reshape((-1,) + (1,) * (len(shape) - 1 - position))
    return level


def centred(stream_key, dims, deviation, most, shards=(), kind=jnp.bfloat16):
    level = level_of(stream_key, dims, shards, -0.22, 0.18) if shards else 1.0
    drawn = jax.random.normal(stream_key, dims, jnp.float32) * deviation * level
    return jnp.minimum(jnp.maximum(drawn, -most), most).astype(kind)


def setup_inputs(seed: int = 0) -> dict:
    key_list = jax.random.split(jax.random.key(seed), 4)
    return {
        "conserved_fields": draw_conserved_fields(jax.random.fold_in(key_list[3], 71), 0),
        "coeff": centred(key_list[1], (2, KXH, 6, NY, NZP), (KXH * NZP // 1024) ** -0.5, 0.25, ((1, 8), (3, 4))),
        "feed_plane": place_ends(jax.random.randint(key_list[2], (FORCE,), 0, NXP), jax.random.fold_in(key_list[2], 1), 0, NXP - 1).astype(jnp.int32),
    }


ADIABATIC_INDEX = 1.4
CAPACITY_CONST = 2.5
OSCILLATOR_SCALE = 2.0
VIBRANT_LAG = 0.5
LANDAU_FIT_LAW = 1.5
SURFACE_DIST_SQ = 0.36
TIME_STEP = 0.05
FORCING_RATE = 2.0
WENO_EPSILON = 1e-06

def caloric_bundle(conserved_fields):
    fluid_rho_field = conserved_fields[0]
    motion_share = 0.5 * (jnp.square(conserved_fields[1]) + jnp.square(conserved_fields[2]) + jnp.square(conserved_fields[3])) / jnp.square(fluid_rho_field)
    translational_kelvin = (conserved_fields[4] / fluid_rho_field - motion_share - conserved_fields[5] / fluid_rho_field) / CAPACITY_CONST
    thermodynamic_stress = fluid_rho_field * translational_kelvin
    return (fluid_rho_field, translational_kelvin, thermodynamic_stress)

def directional(extended_fields, component):
    fluid_rho_field, translational_kelvin, thermodynamic_stress = caloric_bundle(extended_fields)
    crossflow_flux_field = extended_fields[component] / fluid_rho_field
    flux_rows = []
    for member in range(6):
        entry = extended_fields[member] * crossflow_flux_field
        if member == component:
            entry = entry + thermodynamic_stress
        if member == 4:
            entry = entry + thermodynamic_stress * crossflow_flux_field
        flux_rows.append(entry)
    forcing_samples = jnp.abs(crossflow_flux_field) + jnp.sqrt(ADIABATIC_INDEX * translational_kelvin)
    return (jnp.stack(flux_rows), forcing_samples)

def weno_face(minus_two, minus_one, centre, plus_one, plus_two):
    low_poly = (2.0 * minus_two - 7.0 * minus_one + 11.0 * centre) / 6.0
    mid_poly = (-minus_one + 5.0 * centre + 2.0 * plus_one) / 6.0
    high_poly = (2.0 * centre + 5.0 * plus_one - plus_two) / 6.0
    low_beta = 13.0 / 12.0 * jnp.square(minus_two - 2.0 * minus_one + centre) + 0.25 * jnp.square(minus_two - 4.0 * minus_one + 3.0 * centre)
    mid_beta = 13.0 / 12.0 * jnp.square(minus_one - 2.0 * centre + plus_one) + 0.25 * jnp.square(minus_one - plus_one)
    high_beta = 13.0 / 12.0 * jnp.square(centre - 2.0 * plus_one + plus_two) + 0.25 * jnp.square(3.0 * centre - 4.0 * plus_one + plus_two)
    low_weight = 0.1 / jnp.square(WENO_EPSILON + low_beta)
    mid_weight = 0.6 / jnp.square(WENO_EPSILON + mid_beta)
    high_weight = 0.3 / jnp.square(WENO_EPSILON + high_beta)
    return (low_weight * low_poly + mid_weight * mid_poly + high_weight * high_poly) / (low_weight + mid_weight + high_weight)

def sweep_axis(extended_fields, axis, component):
    length = extended_fields.shape[axis] - 6
    fluxes, forcing_samples = directional(extended_fields, component)

    def window(array, offset, dim):
        return lax.slice_in_dim(array, offset, offset + length + 1, axis=dim)
    wave_speed = window(forcing_samples, 0, axis - 1)
    for offset in range(1, 6):
        wave_speed = jnp.maximum(wave_speed, window(forcing_samples, offset, axis - 1))
    wave_speed = wave_speed[None]
    upwind = [0.5 * (window(fluxes, offset, axis) + wave_speed * window(extended_fields, offset, axis)) for offset in range(5)]
    downwind = [0.5 * (window(fluxes, offset, axis) - wave_speed * window(extended_fields, offset, axis)) for offset in (5, 4, 3, 2, 1)]
    face_flux = weno_face(*upwind) + weno_face(*downwind)
    return lax.slice_in_dim(face_flux, 1, length + 1, axis=axis) - lax.slice_in_dim(face_flux, 0, length, axis=axis)

def wall_pad(conserved_fields):
    reflected_fields = conserved_fields[:, :, :, 2::-1]
    translational_kelvin = caloric_bundle(reflected_fields)[1]
    ghost_layer_kelvin = SURFACE_DIST_SQ / translational_kelvin
    ghost_layer_oscillator = reflected_fields[4] - CAPACITY_CONST * reflected_fields[0] * (translational_kelvin - ghost_layer_kelvin)
    ghost_cells = jnp.stack([reflected_fields[0], -reflected_fields[1], -reflected_fields[2], -reflected_fields[3], ghost_layer_oscillator, reflected_fields[5]])
    top_cells = jnp.repeat(conserved_fields[:, :, :, -1:], 3, axis=3)
    return jnp.concatenate([ghost_cells, conserved_fields, top_cells], axis=3)

def relaxation(conserved_fields):
    fluid_rho_field, translational_kelvin, thermodynamic_stress = caloric_bundle(conserved_fields)
    balanced_oscillator_share = OSCILLATOR_SCALE / (jnp.exp(OSCILLATOR_SCALE / translational_kelvin) - 1.0)
    settling_interval = VIBRANT_LAG * jnp.exp(LANDAU_FIT_LAW * (jnp.exp(-jnp.log(translational_kelvin) / 3.0) - 1.0)) / thermodynamic_stress
    return (fluid_rho_field * balanced_oscillator_share - conserved_fields[5]) / settling_interval

def precursor_feed(coeff, feed_plane):
    span_ids = jnp.arange(NZP, dtype=jnp.int32)[:, None] * jnp.arange(NZ, dtype=jnp.int32)[None, :] % NZP
    span_angle = 2.0 * math.pi / NZP * span_ids.astype(jnp.float32)
    span_table = jnp.concatenate([jnp.cos(span_angle), jnp.sin(span_angle)], axis=1).astype(jnp.bfloat16)
    span_table = lax.optimization_barrier(span_table).astype(jnp.float32)
    stream_ids = feed_plane[:, None] * jnp.arange(KXH, dtype=jnp.int32)[None, :] % NXP
    stream_angle = 2.0 * math.pi / NXP * stream_ids.astype(jnp.float32)
    stream_table = jnp.concatenate([jnp.cos(stream_angle), -jnp.sin(stream_angle)], axis=1).astype(jnp.bfloat16)
    stream_table = lax.optimization_barrier(stream_table).astype(jnp.float32)

    def one_variable(block):
        coeff_rows = block.reshape(2 * KXH * NY, NZP).astype(jnp.float32)
        product = jnp.dot(coeff_rows, span_table, precision=lax.Precision.HIGHEST).reshape(2, KXH, NY, 2 * NZ)
        real_part = product[0, :, :, :NZ] - product[1, :, :, NZ:]
        imag_part = product[0, :, :, NZ:] + product[1, :, :, :NZ]
        mixed_modes = jnp.concatenate([real_part, imag_part], axis=0).astype(jnp.bfloat16)
        mixed_modes = lax.optimization_barrier(mixed_modes).astype(jnp.float32)
        summed = jnp.dot(stream_table, mixed_modes.reshape(2 * KXH, NY * NZ), precision=lax.Precision.HIGHEST)
        return summed.reshape(FORCE, NY, NZ)
    feed_values = lax.map(one_variable, jnp.moveaxis(coeff, 2, 0))
    return jnp.transpose(feed_values, (0, 1, 3, 2))

def reference(conserved_fields, coeff, feed_plane):
    stream_pad = jnp.concatenate([jnp.repeat(conserved_fields[:, :1], 3, axis=1), conserved_fields, jnp.repeat(conserved_fields[:, -1:], 3, axis=1)], axis=1)

    def block_rate(start):
        block = lax.dynamic_slice_in_dim(stream_pad, start, CX + 6, axis=1)
        interior = block[:, 3:-3]
        span_pad = jnp.concatenate([interior[:, :, -3:], interior, interior[:, :, :3]], axis=2)
        tendency = -(sweep_axis(block, 1, 1) + sweep_axis(span_pad, 2, 3) + sweep_axis(wall_pad(interior), 3, 2))
        return tendency.at[5].add(relaxation(interior))
    starts = jnp.arange(N_GX, dtype=jnp.int32) * CX
    blocks = lax.map(block_rate, starts)
    tendency = jnp.moveaxis(blocks, 0, 1).reshape(6, NX, NZ, NY)
    target = precursor_feed(coeff, feed_plane)
    plane_pos = jnp.arange(FORCE, dtype=jnp.int32).astype(jnp.float32)
    strength = FORCING_RATE * jnp.square(1.0 - plane_pos / FORCE)
    forcing = strength[None, :, None, None] * (target - conserved_fields[:, :FORCE])
    tendency = tendency.at[:, :FORCE].add(forcing)
    return conserved_fields + TIME_STEP * tendency
```

```python
import functools
import math

import jax
import jax.numpy as jnp
import numpy as np
from jax import lax
from jax.experimental import pallas as pl
from jax.experimental.pallas import tpu as pltpu
from jax.sharding import Mesh, PartitionSpec as P

SUB, LANE = 8, 128
EPS = 3e-6
F32, BF16 = jnp.float32, jnp.bfloat16


def cell_flux(q, comp):
    r, m1, m2, m3, e, ev = q
    rinv = 1.0 / r
    kin = 0.5 * (m1 * m1 + m2 * m2 + m3 * m3) * rinv
    p = 0.4 * (e - kin - ev)
    un = q[comp] * rinv
    c = jnp.sqrt(1.4 * p * rinv)
    flux = [v * un for v in q]
    flux[comp] = flux[comp] + p
    flux[4] = (e + p) * un
    return flux, jnp.abs(un) + c


def correction(gmm, gm, gp, gpp):
    u0 = gmm - 1.375 * gm
    u1 = gm - 0.625 * gp
    u1r = gp - 0.625 * gm
    u2 = gpp - 1.375 * gp
    tm = (0.609375 * gm) * gm + EPS
    tp = (0.609375 * gp) * gp + EPS
    s0 = u0 * u0 + tm
    s1 = u1 * u1 + tp
    s2 = u2 * u2 + tp
    left = u0 + u1r
    right = u2 + u1
    p12 = s1 * s2
    p01 = s0 * s1
    p02 = s0 * s2
    w0 = p12 * p12
    w2 = 3.0 * (p01 * p01)
    w1 = 6.0 * (p02 * p02)
    num = (w0 + w0) * left + w2 * right
    den = w0 + w1 + w2
    return num * pl.reciprocal(den, approx=True)


def sweep(comp, cells, low, mid, high, put, gf_ref, gq_ref, mx_ref):
    def step(j, carry, q):
        flux, s = cell_flux(q, comp)
        pf, pq, ps = carry
        for v in range(6):
            gf_ref[v, j - 1] = flux[v] - pf[v]
            gq_ref[v, j - 1] = q[v] - pq[v]
        mx_ref[j - 1] = jnp.maximum(s, ps)
        return flux, q, s

    q0 = low(0)
    f0, s0 = cell_flux(q0, comp)
    carry = (f0, q0, s0)
    for j in (1, 2):
        carry = step(j, carry, low(j))
    carry = lax.fori_loop(0, cells, lambda j, c: step(j + 3, c, mid(j)), carry)
    for j in range(3):
        carry = step(cells + 3 + j, carry, high(j))

    def face(f):
        a = jnp.maximum(jnp.maximum(mx_ref[f], mx_ref[f + 2]), mx_ref[f + 4])
        out = []
        for v in range(6):
            g = [gf_ref[v, f + k] for k in range(5)]
            h = [a * gq_ref[v, f + k] for k in range(5)]
            up = correction(g[0] + h[0], g[1] + h[1], g[2] + h[2], g[3] + h[3])
            down = correction(g[4] - h[4], g[3] - h[3], g[2] - h[2], g[1] - h[1])
            out.append((h[1] + h[3] - (h[2] + h[2])) + (down - up))
        return out

    def body(f, before):
        after = face(f)
        total = []
        for v in range(6):
            g = [gf_ref[v, f + k] for k in range(4)]
            total.append(7.0 * (g[2] + g[1]) - (g[3] + g[0]) + (after[v] - before[v]))
        put(f - 1, total)
        return after

    lax.fori_loop(1, cells + 1, body, face(0))


def scratch(cells):
    return [
        pltpu.VMEM((6, cells + 5, SUB, LANE), F32),
        pltpu.VMEM((6, cells + 5, SUB, LANE), F32),
        pltpu.VMEM((cells + 5, SUB, LANE), F32),
    ]


def stream_kernel(nx, nz, flags, q_ref, lo_ref, hi_ref, acc_ref, gf, gq, mx):
    first, last = flags[0] == 1, flags[1] == 1

    @pl.loop(0, nz // SUB)
    def _(t):
        base = pl.multiple_of(t * SUB, SUB)

        def mid(j):
            return [q_ref[pl.ds(pl.multiple_of((v * nx + j) * nz + base, SUB), SUB), :] for v in range(6)]

        def side(ref, flag, edge):
            def load(j):
                return [
                    jnp.where(flag, e, ref[pl.ds(pl.multiple_of((v * 3 + j) * nz + base, SUB), SUB), :])
                    for v, e in enumerate(mid(edge))
                ]
            return load

        def put(c, total):
            for v in range(6):
                acc_ref[pl.ds(pl.multiple_of((v * nx + c) * nz + base, SUB), SUB), :] = total[v]

        sweep(1, nx, side(lo_ref, first, 0), mid, side(hi_ref, last, nx - 1), put, gf, gq, mx)


def span_kernel(nx, nz, q_ref, lo_ref, hi_ref, acc_in, acc_ref, gf, gq, mx):
    @pl.loop(0, nx // SUB)
    def _(t):
        base = t * (SUB * nz)
        hbase = pl.multiple_of(t * SUB, SUB)

        def rows(v, j):
            return pl.ds(v * nx * nz + base + j, SUB, stride=nz)

        def mid(j):
            return [q_ref[rows(v, j), :] for v in range(6)]

        def side(ref):
            def load(j):
                return [ref[pl.ds(pl.multiple_of((v * 3 + j) * nx + hbase, SUB), SUB), :] for v in range(6)]
            return load

        def put(c, total):
            for v in range(6):
                acc_ref[rows(v, c), :] = acc_in[rows(v, c), :] + total[v]

        sweep(3, nz, side(lo_ref), mid, side(hi_ref), put, gf, gq, mx)


def wall_kernel(nx, nz, ny, strength, q_ref, acc_in, out_ref, yq, yt, gf, gq, mx):
    seg = ny // SUB
    cells = nx * nz

    @pl.loop(0, cells // LANE)
    def _(t):
        base = pl.multiple_of(t * LANE, LANE)
        for v in range(6):
            block = q_ref[pl.ds(pl.multiple_of(v * cells + base, LANE), LANE), :]
            yq[v, SUB : SUB + ny] = block.T
        q = [yq[v, SUB : 2 * SUB] for v in range(6)]
        rinv = 1.0 / q[0]
        temp = 0.4 * (q[4] - 0.5 * (q[1] * q[1] + q[2] * q[2] + q[3] * q[3]) * rinv - q[5]) * rinv
        ghost = [q[0], -q[1], -q[2], -q[3], q[4] - 2.5 * q[0] * (temp - 0.36 / temp), q[5]]
        for v in range(6):
            top = yq[v, SUB + ny - 1 : SUB + ny]
            for j in range(3):
                yq[v, SUB - 1 - j : SUB - j] = ghost[v][j : j + 1]
                yq[v, SUB + ny + j : SUB + ny + j + 1] = top

        def load(j):
            return [yq[v, pl.ds(SUB + j, SUB, stride=seg), :] for v in range(6)]

        def put(c, total):
            for v in range(6):
                yt[v, pl.ds(c, SUB, stride=seg), :] = total[v]

        sweep(2, seg, lambda j: load(j - 3), load, lambda j: load(seg + j), put, gf, gq, mx)

        for v in range(6):
            yt[v] = yt[v].T

        @pl.loop(0, LANE // SUB)
        def _(i):
            o = pl.multiple_of(i * SUB, SUB)
            rows = [pl.ds(pl.multiple_of(v * cells + base + o, SUB), SUB) for v in range(6)]
            q = [q_ref[rows[v], :] for v in range(6)]
            rinv = 1.0 / q[0]
            p = 0.4 * (q[4] - 0.5 * (q[1] * q[1] + q[2] * q[2] + q[3] * q[3]) * rinv - q[5])
            temp = p * rinv
            share = 2.0 / (jnp.exp(2.0 / temp) - 1.0)
            lag = jnp.exp(1.5 * (jnp.exp(-jnp.log(temp) / 3.0) - 1.0))
            relax = (q[0] * share - q[5]) * (2.0 * p) / lag
            pull = strength[(base + o) // nz]
            for v in range(6):
                rate = (acc_in[rows[v], :] + yt[v, pl.ds(o, SUB), :]) * (-1.0 / 12.0)
                if v == 5:
                    rate = rate + relax
                out_ref[rows[v], :] = q[v] + 0.05 * (rate - pull * q[v])


VM = pl.BlockSpec(memory_space=pltpu.VMEM)


def cost(n):
    return pl.CostEstimate(flops=n * 4000, bytes_accessed=n * 60, transcendentals=n * 12)


def params():
    return pltpu.CompilerParams(vmem_limit_bytes=40 * 2**20)


def rhs(q, xlo, xhi, zlo, zhi, edges, strength):
    _, nx, nz, ny = q.shape
    flat = q.reshape(6 * nx * nz, ny)
    shape = jax.ShapeDtypeStruct(flat.shape, F32)
    acc = pl.pallas_call(
        functools.partial(stream_kernel, nx, nz), out_shape=shape, name="stream_sweep",
        in_specs=[pl.BlockSpec(memory_space=pltpu.SMEM), VM, VM, VM], out_specs=VM,
        scratch_shapes=scratch(nx), compiler_params=params(), cost_estimate=cost(nx * nz * ny),
    )(edges, flat, xlo.reshape(-1, ny), xhi.reshape(-1, ny))
    acc = pl.pallas_call(
        functools.partial(span_kernel, nx, nz), out_shape=shape, name="span_sweep",
        in_specs=[VM] * 4, out_specs=VM,
        scratch_shapes=scratch(nz), compiler_params=params(), cost_estimate=cost(nx * nz * ny),
    )(flat, zlo.reshape(-1, ny), zhi.reshape(-1, ny), acc)
    out = pl.pallas_call(
        functools.partial(wall_kernel, nx, nz, ny), out_shape=shape, name="wall_sweep",
        in_specs=[pl.BlockSpec(memory_space=pltpu.SMEM), VM, VM], out_specs=VM,
        scratch_shapes=[pltpu.VMEM((6, ny + 2 * SUB, LANE), F32), pltpu.VMEM((6, ny, LANE), F32)] + scratch(ny // SUB),
        compiler_params=params(), cost_estimate=cost(nx * nz * ny),
    )(strength, flat, acc)
    return out.reshape(q.shape)


def span_tables(modes, points):
    ids = np.arange(modes)[:, None] * np.arange(points)[None, :] % modes
    angle = 2.0 * np.pi / modes * ids
    cz, sz = np.cos(angle), np.sin(angle)
    return jnp.asarray(np.concatenate([np.concatenate([cz, sz], 1), np.concatenate([-sz, cz], 1)], 0), F32).astype(BF16)


def feed_kernel(planes, parts, z_ref, rep_ref, coeff_ref, out_ref, rhs_ref, acc_ref):
    _, kc, levels, modes = coeff_ref.shape
    groups = levels // SUB
    points = z_ref.shape[1] // 2
    rows = rep_ref.shape[1]
    step = pl.program_id(1)
    prod = jnp.dot(coeff_ref[0].reshape(kc * levels, modes), z_ref[:modes], preferred_element_type=F32)
    prod += jnp.dot(coeff_ref[1].reshape(kc * levels, modes), z_ref[modes:], preferred_element_type=F32)
    prod = prod.reshape(kc, groups, SUB, 2 * points)
    for g in range(groups):
        part = prod[:, g].reshape(kc * SUB, 2 * points).astype(BF16)
        for c in range(2):
            rhs_ref[c * kc * SUB : (c + 1) * kc * SUB, g * points : (g + 1) * points] = part[:, c * points : (c + 1) * points]
    width = kc * SUB
    own = lax.broadcasted_iota(jnp.int32, (rows, SUB, width), 2) % SUB == lax.broadcasted_iota(jnp.int32, (rows, SUB, width), 1)
    left = jnp.concatenate(
        [jnp.where(own, rep_ref[c][:, None, :], 0.0).reshape(rows * SUB, width) for c in range(2)], axis=1
    ).astype(BF16)
    total = jnp.dot(left, rhs_ref[...], preferred_element_type=F32)

    @pl.when(step == 0)
    def _():
        acc_ref[...] = total

    @pl.when(step > 0)
    def _():
        acc_ref[...] += total

    @pl.when(step == pl.num_programs(1) - 1)
    def _():
        per = LANE // levels
        piece = points // parts
        for t in range(rows // per):
            tile = jnp.concatenate(
                [
                    acc_ref[f * SUB : (f + 1) * SUB, g * points : (g + 1) * points]
                    for f in range(t * per, (t + 1) * per)
                    for g in range(groups)
                ],
                axis=0,
            )
            turned = tile.T
            for s in range(parts):
                out_ref[s, t] = turned[s * piece : (s + 1) * piece]


def feed(coeff, rep, table, first, count, parts, chunk):
    _, modes_x, variables, levels, modes = coeff.shape
    points = table.shape[1] // 2
    rows = rep.shape[1]
    groups = levels // SUB
    tiles = rows * levels // LANE
    chunk = min(chunk, modes_x)
    flops = 2 * count * modes_x * levels * (2 * modes * 2 * points + rows * SUB * 2 * points)
    return pl.pallas_call(
        functools.partial(feed_kernel, rows, parts), name="feed",
        out_shape=jax.ShapeDtypeStruct((count, parts, tiles, points // parts, LANE), F32),
        grid=(count, modes_x // chunk),
        in_specs=[
            pl.BlockSpec(table.shape, lambda v, k: (0, 0)),
            pl.BlockSpec((2, rows, chunk * SUB), lambda v, k: (0, 0, k)),
            pl.BlockSpec((2, chunk, None, levels, modes), lambda v, k: (0, k, first + v, 0, 0)),
        ],
        out_specs=pl.BlockSpec((None, parts, tiles, points // parts, LANE), lambda v, k: (v, 0, 0, 0, 0)),
        scratch_shapes=[
            pltpu.VMEM((2 * chunk * SUB, groups * points), BF16),
            pltpu.VMEM((rows * SUB, groups * points), F32),
        ],
        compiler_params=pltpu.CompilerParams(vmem_limit_bytes=40 * 2**20),
        cost_estimate=pl.CostEstimate(flops=flops, bytes_accessed=2 * count * modes_x * levels * modes * 2, transcendentals=0),
    )(table, rep, coeff)


def factors(feed_plane, mode_first, modes_x, stream_points, levels):
    per = LANE // levels
    planes = feed_plane.shape[0]
    rows = -(-planes // per) * per
    padded = jnp.concatenate([feed_plane, jnp.zeros((rows - planes,), jnp.int32)])
    ids = mode_first + lax.broadcasted_iota(jnp.int32, (rows, modes_x * SUB), 1) // SUB
    angle = 2.0 * math.pi / stream_points * (padded[:, None] * ids % stream_points).astype(F32)
    rep = jnp.stack([jnp.cos(angle), -jnp.sin(angle)])
    return rep.astype(BF16).astype(F32)


def force_kernel(per, levels, offset, strength, *refs):
    targets, state, out_ref = refs[:-2], refs[-2], refs[-1]
    parts = targets[0].shape[0]
    first = pl.program_id(0) * per
    lane = lax.broadcasted_iota(jnp.int32, targets[0].shape[1:], 1)
    for v, target in enumerate(targets):
        blocks = [target[s] for s in range(parts)]
        for i in range(per):
            row = blocks[0] if i == 0 else pltpu.roll(blocks[0], (-i * levels) % LANE, 1)
            for s in range(1, parts):
                moved = blocks[s] if s == i else pltpu.roll(blocks[s], ((s - i) * levels) % LANE, 1)
                row = jnp.where(lane >= s * levels, moved, row)
            out_ref[v, i] = state[v, i] + (0.05 * strength[first + i]) * row


def force(state, targets, strength, offset, levels, planes):
    variables, nx, nz, ny = state.shape
    per = LANE // levels
    parts, tiles = targets[0].shape[:2]
    steps = -(-min(planes, nx) // per)

    def tile(t, offset, strength):
        return (0, jnp.minimum(t + offset[0], tiles - 1), 0, 0)

    def plane(t, offset, strength):
        return (0, t, 0, 0)

    blocks = [pl.BlockSpec((parts, None, nz, LANE), tile)] * variables
    cells = pl.BlockSpec((variables, per, nz, ny), plane)
    return pl.pallas_call(
        functools.partial(force_kernel, per, levels), name="force",
        out_shape=jax.ShapeDtypeStruct(state.shape, F32),
        grid_spec=pltpu.PrefetchScalarGridSpec(
            num_scalar_prefetch=2, grid=(steps,), in_specs=blocks + [cells], out_specs=cells),
        input_output_aliases={2 + variables: 0},
        compiler_params=pltpu.CompilerParams(vmem_limit_bytes=20 * 2**20),
    )(offset, strength, *targets, state)


GX = ("gh", "gl")


def local(state, coeff, feed_plane):
    high, pair, parts = lax.axis_size("gh"), lax.axis_size("gl"), lax.axis_size("gz")
    gx = high * pair
    me = lax.axis_index("gh") * pair + lax.axis_index("gl")
    variables, nx, nz, ny = state.shape
    _, modes_x, _, levels, modes = coeff.shape
    planes = feed_plane.shape[0]

    ring = [(i, (i + 1) % parts) for i in range(parts)]
    line = [(i, i + 1) for i in range(gx - 1)]
    zside = [jnp.transpose(state[:, :, k], (0, 2, 1, 3)) for k in (slice(nz - 3, nz), slice(0, 3))]
    xlo = lax.ppermute(state[:, nx - 3 :], GX, line)
    xhi = lax.ppermute(state[:, :3], GX, [(j, i) for i, j in line])
    zlo = lax.ppermute(zside[0], "gz", ring)
    zhi = lax.ppermute(zside[1], "gz", [(j, i) for i, j in ring])

    rep = factors(feed_plane, me * modes_x, modes_x, 2 * modes_x * gx, levels)
    table = span_tables(modes, nz * parts)
    targets = []
    for first in range(0, variables, pair):
        part = feed(coeff, rep, table, first, pair, parts, 32)
        part = lax.all_to_all(part.reshape(-1, *part.shape[2:]), ("gl", "gz"), split_axis=0, concat_axis=0, tiled=True)
        part = part.reshape(pair, parts, *part.shape[1:]).sum(0)
        stride = 1
        while stride < high:
            hops = [(i, i - stride) for i in range(stride, high, 2 * stride)]
            part = part + lax.ppermute(part, "gh", hops)
            stride *= 2
        owned = [part] + [lax.ppermute(part, GX, [(i, 0)]) for i in range(1, pair)]
        for other in range(1, -(-planes // nx)):
            owned = [jnp.where(me == other, lax.ppermute(t, GX, [(0, other)]), t) for t in owned]
        targets += owned

    edges = jnp.stack([me == 0, me == gx - 1]).astype(jnp.int32)
    plane = me * nx + jnp.arange(nx, dtype=jnp.int32)
    strength = jnp.where(plane < planes, 2.0 * jnp.square(1.0 - plane.astype(F32) / planes), 0.0)
    new = rhs(state, xlo, xhi, zlo, zhi, edges, strength)
    offset = jnp.reshape(me * nx // (LANE // levels), (1,))
    return force(new, targets, strength, offset, levels, planes)


def solution(mesh):
    gx, gz = mesh.devices.shape
    pair = 2 if gx % 2 == 0 else 1
    split = Mesh(mesh.devices.reshape(gx // pair, pair, gz), ("gh", "gl", "gz"))
    cells = P(None, GX, "gz", None)
    return jax.shard_map(
        local, mesh=split, in_specs=(cells, P(None, GX, None, "gz", None), P()), out_specs=cells, check_vma=False
    )
```

```python
import functools
import math

import jax
import jax.numpy as jnp
import numpy as np
from jax import lax
from jax.experimental import pallas as pl
from jax.experimental.pallas import tpu as pltpu
from jax.sharding import Mesh, PartitionSpec as P

SUB, LANE = 8, 128
EPS = 3e-6
F32, BF16 = jnp.float32, jnp.bfloat16


U1, U2 = 16, 4
TALL = 64


def cell_flux(q, comp):
    r, m1, m2, m3, e, ev = q
    rinv = 1.0 / r
    kin = 0.5 * (m1 * m1 + m2 * m2 + m3 * m3) * rinv
    p = 0.4 * (e - kin - ev)
    un = q[comp] * rinv
    c = jnp.sqrt(1.4 * p * rinv)
    flux = [v * un for v in q]
    flux[comp] = flux[comp] + p
    flux[4] = (e + p) * un
    return flux, jnp.abs(un) + c


def correction(gmm, gm, gp, gpp):
    u0 = gmm - 1.375 * gm
    u1 = gm - 0.625 * gp
    u1r = gp - 0.625 * gm
    u2 = gpp - 1.375 * gp
    tm = (0.609375 * gm) * gm + EPS
    tp = (0.609375 * gp) * gp + EPS
    s0 = u0 * u0 + tm
    s1 = u1 * u1 + tp
    s2 = u2 * u2 + tp
    left = u0 + u1r
    right = u2 + u1
    p12 = s1 * s2
    p01 = s0 * s1
    p02 = s0 * s2
    w0 = p12 * p12
    w2 = 3.0 * (p01 * p01)
    w1 = 6.0 * (p02 * p02)
    num = (w0 + w0) * left + w2 * right
    den = w0 + w1 + w2
    return num * pl.reciprocal(den, approx=True)


def sweep(comp, cells, low, mid, high, put, gf_ref, gq_ref, mx_ref):
    def step(j, carry, q):
        flux, s = cell_flux(q, comp)
        pf, pq, ps = carry
        for v in range(6):
            gf_ref[v, j - 1] = flux[v] - pf[v]
            gq_ref[v, j - 1] = q[v] - pq[v]
        mx_ref[j - 1] = jnp.maximum(s, ps)
        return flux, q, s

    q0 = low(0)
    f0, s0 = cell_flux(q0, comp)
    carry = (f0, q0, s0)
    for j in (1, 2):
        carry = step(j, carry, low(j))
    carry = lax.fori_loop(0, cells, lambda j, c: step(j + 3, c, mid(j)), carry, unroll=U1)
    for j in range(3):
        carry = step(cells + 3 + j, carry, high(j))

    def face(f):
        a = jnp.maximum(jnp.maximum(mx_ref[f], mx_ref[f + 2]), mx_ref[f + 4])
        out = []
        for v in range(6):
            g = [gf_ref[v, f + k] for k in range(5)]
            h = [a * gq_ref[v, f + k] for k in range(5)]
            up = correction(g[0] + h[0], g[1] + h[1], g[2] + h[2], g[3] + h[3])
            down = correction(g[4] - h[4], g[3] - h[3], g[2] - h[2], g[1] - h[1])
            out.append((h[1] + h[3] - (h[2] + h[2])) + (down - up))
        return out

    def body(f, before):
        after = face(f)
        total = []
        for v in range(6):
            g = [gf_ref[v, f + k] for k in range(4)]
            total.append(7.0 * (g[2] + g[1]) - (g[3] + g[0]) + (after[v] - before[v]))
        put(f - 1, total)
        return after

    lax.fori_loop(1, cells + 1, body, face(0), unroll=U2)


def scratch(cells):
    return [
        pltpu.VMEM((6, cells + 5, SUB, LANE), F32),
        pltpu.VMEM((6, cells + 5, SUB, LANE), F32),
        pltpu.VMEM((cells + 5, SUB, LANE), F32),
    ]


def stream_kernel(flags, q_ref, lo_ref, hi_ref, acc_ref, gf, gq, mx):
    nx = q_ref.shape[1]

    def mid(j):
        return [q_ref[v, j] for v in range(6)]

    def side(ref, flag, edge):
        def load(j):
            return [jnp.where(flag == 1, e, ref[v, j]) for v, e in enumerate(mid(edge))]
        return load

    def put(c, total):
        for v in range(6):
            acc_ref[v, c] = total[v]

    sweep(1, nx, side(lo_ref, flags[0], 0), mid, side(hi_ref, flags[1], nx - 1), put, gf, gq, mx)


def span_kernel(nz, q_ref, lo_ref, hi_ref, acc_in, acc_ref, gf, gq, mx):
    def rows(j):
        return pl.ds(j, SUB, stride=nz)

    def mid(j):
        return [q_ref[v, rows(j), :] for v in range(6)]

    def side(ref):
        return lambda j: [ref[j, v] for v in range(6)]

    def put(c, total):
        for v in range(6):
            acc_ref[v, rows(c), :] = acc_in[v, rows(c), :] + total[v]

    sweep(3, nz, side(lo_ref), mid, side(hi_ref), put, gf, gq, mx)


def wall_kernel(nz, strength, q_ref, acc_in, out_ref, yq, yt, gf, gq, mx):
    ny = q_ref.shape[2]
    seg = ny // SUB
    for v in range(6):
        yq[v, SUB : SUB + ny] = q_ref[v].T
    q = [yq[v, SUB : 2 * SUB] for v in range(6)]
    rinv = 1.0 / q[0]
    temp = 0.4 * (q[4] - 0.5 * (q[1] * q[1] + q[2] * q[2] + q[3] * q[3]) * rinv - q[5]) * rinv
    ghost = [q[0], -q[1], -q[2], -q[3], q[4] - 2.5 * q[0] * (temp - 0.36 / temp), q[5]]
    for v in range(6):
        top = yq[v, SUB + ny - 1 : SUB + ny]
        for j in range(3):
            yq[v, SUB - 1 - j : SUB - j] = ghost[v][j : j + 1]
            yq[v, SUB + ny + j : SUB + ny + j + 1] = top

    def load(j):
        return [yq[v, pl.ds(SUB + j, SUB, stride=seg), :] for v in range(6)]

    def put(c, total):
        for v in range(6):
            yt[v, pl.ds(c, SUB, stride=seg), :] = total[v]

    sweep(2, seg, lambda j: load(j - 3), load, lambda j: load(seg + j), put, gf, gq, mx)

    for v in range(6):
        yt[v] = yt[v].T

    @pl.loop(0, LANE // TALL)
    def _(i):
        o = pl.multiple_of(i * TALL, TALL)
        rows = pl.ds(o, TALL)
        q = [q_ref[v, rows, :] for v in range(6)]
        rinv = 1.0 / q[0]
        p = 0.4 * (q[4] - 0.5 * (q[1] * q[1] + q[2] * q[2] + q[3] * q[3]) * rinv - q[5])
        temp = p * rinv
        share = 2.0 / (jnp.exp(2.0 / temp) - 1.0)
        lag = jnp.exp(1.5 * (jnp.exp(-jnp.log(temp) / 3.0) - 1.0))
        relax = (q[0] * share - q[5]) * (2.0 * p) / lag
        pull = jnp.zeros((TALL, ny), F32)
        for k in range(TALL // nz):
            pull = jnp.where(lax.broadcasted_iota(jnp.int32, (TALL, ny), 0) >= k * nz, strength[(pl.program_id(0) * LANE + o) // nz + k], pull)
        for v in range(6):
            rate = (acc_in[v, rows, :] + yt[v, rows, :]) * (-1.0 / 12.0)
            if v == 5:
                rate = rate + relax
            out_ref[v, rows, :] = q[v] + 0.05 * (rate - pull * q[v])


def far(x):
    return pltpu.with_memory_space_constraint(x, pltpu.HBM)


def call(kernel, name, q, grid, in_specs, out_spec, shapes):
    return pl.pallas_call(
        kernel, out_shape=pltpu.HBM(q.shape, F32), name=name, grid=(grid,), in_specs=in_specs, out_specs=out_spec,
        scratch_shapes=shapes, compiler_params=pltpu.CompilerParams(vmem_limit_bytes=16 * 2**20),
        cost_estimate=pl.CostEstimate(flops=q.size * 700, bytes_accessed=q.size * 8, transcendentals=q.size * 2),
    )


SCALARS = pl.BlockSpec(memory_space=pltpu.SMEM)


def stream_sweep(q, xlo, xhi, edges):
    _, nx, nz, ny = q.shape
    cells = pl.BlockSpec((6, nx, SUB, ny), lambda t: (0, 0, t, 0))
    side = pl.BlockSpec((6, 3, SUB, ny), lambda t: (0, 0, t, 0))
    return call(stream_kernel, "stream_sweep", q, nz // SUB, [SCALARS, cells, side, side], cells, scratch(nx))(
        edges, far(q), xlo, xhi)


def span_sweep(q, zlo, zhi, acc):
    _, nx, nz, ny = q.shape
    flat = q.reshape(6, nx * nz, ny)
    cells = pl.BlockSpec((6, SUB * nz, ny), lambda t: (0, t, 0))
    side = pl.BlockSpec((3, 6, SUB, ny), lambda t: (0, 0, t, 0))
    return call(functools.partial(span_kernel, nz), "span_sweep", flat, nx // SUB, [cells, side, side, cells], cells, scratch(nz))(
        far(flat), zlo, zhi, far(acc.reshape(flat.shape))).reshape(q.shape)


def wall_sweep(q, acc, strength):
    _, nx, nz, ny = q.shape
    flat = q.reshape(6, nx * nz, ny)
    cells = pl.BlockSpec((6, LANE, ny), lambda t: (0, t, 0))
    shapes = [pltpu.VMEM((6, ny + 2 * SUB, LANE), F32), pltpu.VMEM((6, ny, LANE), F32)] + scratch(ny // SUB)
    return call(functools.partial(wall_kernel, nz), "wall_sweep", flat, nx * nz // LANE, [SCALARS, cells, cells], cells, shapes)(
        strength, far(flat), far(acc.reshape(flat.shape))).reshape(q.shape)


def span_tables(modes, points):
    ids = np.arange(modes)[:, None] * np.arange(points)[None, :] % modes
    angle = 2.0 * np.pi / modes * ids
    cz, sz = np.cos(angle), np.sin(angle)
    return jnp.asarray(np.concatenate([np.concatenate([cz, sz], 1), np.concatenate([-sz, cz], 1)], 0), F32).astype(BF16)


def feed_kernel(first, count, chunk, depth, rep_ref, z_ref, coeff_ref, out_ref, buf, left_ref, rhs_ref, acc_ref, sems):
    _, modes_x, _, levels, modes = coeff_ref.shape
    groups = levels // SUB
    points = z_ref.shape[1] // 2
    rows = rep_ref.shape[1]
    steps = modes_x // chunk
    total = count * steps
    width = chunk * SUB
    sub = min(8, chunk)

    def copies(n, slot):
        k, v = lax.rem(n, steps) * chunk, first + lax.div(n, steps)
        return [
            pltpu.make_async_copy(coeff_ref.at[c, pl.ds(k, chunk), v], buf.at[slot, c], sems.at[slot, c]) for c in range(2)
        ]

    for n in range(min(depth - 1, total)):
        for copy in copies(n, n):
            copy.start()

    own = lax.broadcasted_iota(jnp.int32, (rows, SUB, width), 2) % SUB == lax.broadcasted_iota(
        jnp.int32, (rows, SUB, width), 1
    )
    for k in range(steps):
        for c in range(2):
            spread = jnp.where(own, rep_ref[c, :, k * width : (k + 1) * width][:, None, :], 0.0)
            left_ref[k, :, c * width : (c + 1) * width] = spread.reshape(rows * SUB, width).astype(BF16)

    def body(n, _):
        slot = lax.rem(n, depth)
        ahead = n + depth - 1

        @pl.when(ahead < total)
        def _():
            for copy in copies(ahead, lax.rem(ahead, depth)):
                copy.start()

        for copy in copies(n, slot):
            copy.wait()
        for i in range(0, chunk, sub):
            both = jnp.concatenate([buf[slot, c, i : i + sub].reshape(sub * levels, modes) for c in range(2)], axis=1)
            prod = jnp.dot(both, z_ref[...], preferred_element_type=F32).reshape(sub, groups, SUB, 2 * points)
            for g in range(groups):
                part = prod[:, g].reshape(sub * SUB, 2 * points).astype(BF16)
                for c in range(2):
                    row = c * width + i * SUB
                    rhs_ref[row : row + sub * SUB, g * points : (g + 1) * points] = part[:, c * points : (c + 1) * points]
        k = lax.rem(n, steps)
        term = jnp.dot(left_ref[k], rhs_ref[...], preferred_element_type=F32)
        acc_ref[...] = jnp.where(k == 0, 0.0, acc_ref[...]) + term

        @pl.when(k == steps - 1)
        def _():
            v = lax.div(n, steps)
            per = LANE // levels
            blocks, parts = out_ref.shape[:2]
            piece = points // parts
            short = piece // blocks
            for t in range(rows // per):
                tile = jnp.concatenate(
                    [
                        acc_ref[f * SUB : (f + 1) * SUB, g * points : (g + 1) * points]
                        for f in range(t * per, (t + 1) * per)
                        for g in range(groups)
                    ],
                    axis=0,
                )
                turned = tile.T
                for s in range(parts):
                    for b in range(blocks):
                        low = s * piece + b * short
                        out_ref[b, s, v, t] = turned[low : low + short]

        return 0

    lax.fori_loop(0, total, body, 0)


def feed(coeff, rep, table, first, count, blocks, parts, chunk, depth):
    _, modes_x, _, levels, modes = coeff.shape
    points = table.shape[1] // 2
    rows = rep.shape[1]
    groups = levels // SUB
    tiles = rows * levels // LANE
    chunk = min(chunk, modes_x)
    steps = modes_x // chunk
    flops = 2 * count * modes_x * levels * (2 * modes * 2 * points + rows * SUB * 2 * points)
    vmem = pl.BlockSpec(memory_space=pltpu.VMEM)
    return pl.pallas_call(
        functools.partial(feed_kernel, first, count, chunk, depth), name="feed",
        out_shape=jax.ShapeDtypeStruct((blocks, parts, count, tiles, points // parts // blocks, LANE), F32),
        in_specs=[vmem, vmem, pl.BlockSpec(memory_space=pl.ANY)], out_specs=vmem,
        scratch_shapes=[
            pltpu.VMEM((depth, 2, chunk, levels, modes), BF16),
            pltpu.VMEM((steps, rows * SUB, 2 * chunk * SUB), BF16),
            pltpu.VMEM((2 * chunk * SUB, groups * points), BF16),
            pltpu.VMEM((rows * SUB, groups * points), F32),
            pltpu.SemaphoreType.DMA((depth, 2)),
        ],
        compiler_params=pltpu.CompilerParams(vmem_limit_bytes=24 * 2**20),
        cost_estimate=pl.CostEstimate(flops=flops, bytes_accessed=2 * count * modes_x * levels * modes * 2, transcendentals=0),
    )(rep, table, coeff)


def factors(feed_plane, mode_first, modes_x, stream_points, levels):
    per = LANE // levels
    planes = feed_plane.shape[0]
    rows = -(-planes // per) * per
    padded = jnp.concatenate([feed_plane, jnp.zeros((rows - planes,), jnp.int32)])
    ids = mode_first + lax.broadcasted_iota(jnp.int32, (rows, modes_x * SUB), 1) // SUB
    angle = 2.0 * math.pi / stream_points * (padded[:, None] * ids % stream_points).astype(F32)
    rep = jnp.stack([jnp.cos(angle), -jnp.sin(angle)])
    return rep.astype(BF16).astype(F32)


def force_kernel(steps, per, levels, owners, offset, strength, *refs):
    far, state, out_ref = refs[:owners], refs[owners], refs[owners + 1]
    near, cells, sems = refs[owners + 2 : 2 * owners + 2], refs[-2], refs[-1]
    parts, variables, tiles, short, _ = near[0].shape

    def planes(t):
        return pl.ds(t * per, per)

    loads = [pltpu.make_async_copy(far[b], near[b], sems.at[b]) for b in range(owners)]
    reads = [pltpu.make_async_copy(state.at[:, planes(t)], cells.at[:, planes(t)], sems.at[owners + t]) for t in range(steps)]
    writes = [
        pltpu.make_async_copy(cells.at[:, planes(t)], out_ref.at[:, planes(t)], sems.at[owners + steps + t])
        for t in range(steps)
    ]
    for copy in loads + reads:
        copy.start()
    for copy in loads:
        copy.wait()
    lane = lax.broadcasted_iota(jnp.int32, (short, LANE), 1)
    for t in range(steps):
        reads[t].wait()
        tile = jnp.minimum(t + offset[0], tiles - 1)

        @pl.loop(0, variables)
        def _(v):
            for b in range(owners):
                blocks = [near[b][s, v, tile] for s in range(parts)]
                for i in range(per):
                    row = blocks[0] if i == 0 else pltpu.roll(blocks[0], (-i * levels) % LANE, 1)
                    for s in range(1, parts):
                        moved = blocks[s] if s == i else pltpu.roll(blocks[s], ((s - i) * levels) % LANE, 1)
                        row = jnp.where(lane >= s * levels, moved, row)
                    some = pl.ds(b * short, short)
                    cells[v, t * per + i, some] = cells[v, t * per + i, some] + (0.05 * strength[t * per + i]) * row

        writes[t].start()
    for copy in writes:
        copy.wait()


def force(state, targets, strength, offset, levels, planes):
    variables, nx, nz, ny = state.shape
    per = LANE // levels
    steps = -(-min(planes, nx) // per)
    owners = len(targets)
    anywhere = pl.BlockSpec(memory_space=pl.ANY)
    return pl.pallas_call(
        functools.partial(force_kernel, steps, per, levels, owners), name="force",
        out_shape=jax.ShapeDtypeStruct(state.shape, F32),
        in_specs=[SCALARS, SCALARS] + [anywhere] * (owners + 1), out_specs=anywhere,
        scratch_shapes=[pltpu.VMEM(t.shape, F32) for t in targets]
        + [pltpu.VMEM((variables, steps * per, nz, ny), F32), pltpu.SemaphoreType.DMA((owners + 2 * steps,))],
        input_output_aliases={2 + owners: 0},
        compiler_params=pltpu.CompilerParams(vmem_limit_bytes=16 * 2**20),
    )(offset, strength, *targets, state)


GX = ("gh", "gl")
LATE = 3


def local(state, coeff, feed_plane):
    high, low, parts = lax.axis_size("gh"), lax.axis_size("gl"), lax.axis_size("gz")
    gx = high * low
    me = lax.axis_index("gh") * low + lax.axis_index("gl")
    variables, nx, nz, ny = state.shape
    _, modes_x, _, levels, modes = coeff.shape
    planes = feed_plane.shape[0]

    ring = [(i, (i + 1) % parts) for i in range(parts)]
    line = [(i, i + 1) for i in range(gx - 1)]
    zside = [jnp.stack([state[:, :, k + j] for j in range(3)]) for k in (nz - 3, 0)]
    xlo = lax.ppermute(state[:, nx - 3 :], GX, line)
    xhi = lax.ppermute(state[:, :3], GX, [(j, i) for i, j in line])
    zlo = lax.ppermute(zside[0], "gz", ring)
    zhi = lax.ppermute(zside[1], "gz", [(j, i) for i, j in ring])

    rep = factors(feed_plane, me * modes_x, modes_x, 2 * modes_x * gx, levels)
    table = span_tables(modes, nz * parts)
    edges = jnp.stack([me == 0, me == gx - 1]).astype(jnp.int32)
    plane = me * nx + jnp.arange(nx, dtype=jnp.int32)
    strength = jnp.where(plane < planes, 2.0 * jnp.square(1.0 - plane.astype(F32) / planes), 0.0)

    def spread(part):
        part = part.reshape(-1, *part.shape[2:])
        part = lax.all_to_all(part, ("gl", "gz"), split_axis=0, concat_axis=0, tiled=True)
        return part.reshape(low, parts, *part.shape[1:]).sum(0)

    def gather(part):
        stride = 1
        while stride < high:
            hops = [(i, i - stride) for i in range(stride, high, 2 * stride)]
            part = part + lax.ppermute(part, "gh", hops)
            stride *= 2
        return part

    early = variables - LATE
    one = feed(coeff, rep, table, 0, early, low, parts, 64, 3)
    one, xlo, xhi, zlo, zhi, rep = lax.optimization_barrier((one, xlo, xhi, zlo, zhi, rep))
    one = spread(one)
    two = feed(coeff, rep, table, early, LATE, low, parts, 64, 3)
    one, two, xlo = lax.optimization_barrier((one, two, xlo))
    one = gather(one)
    two = spread(two)
    acc = stream_sweep(state, xlo, xhi, edges)
    one, two, acc = lax.optimization_barrier((one, two, acc))
    two = gather(two)
    acc = span_sweep(state, zlo, zhi, acc)
    part = jnp.concatenate([one, two], axis=1)
    part, acc = lax.optimization_barrier((part, acc))
    owned = [part] + [lax.ppermute(part, GX, [(i, 0)]) for i in range(1, low)]
    new = wall_sweep(state, acc, strength)
    for other in range(1, -(-planes // nx)):
        owned = [jnp.where(me == other, lax.ppermute(t, GX, [(0, other)]), t) for t in owned]
    offset = jnp.reshape(me * nx // (LANE // levels), (1,))
    return force(new, owned, strength, offset, levels, planes)


def solution(mesh):
    gx, gz = mesh.devices.shape
    low = next(n for n in (4, 2, 1) if gx % n == 0)
    split = Mesh(mesh.devices.reshape(gx // low, low, gz), ("gh", "gl", "gz"))
    cells = P(None, GX, "gz", None)
    return jax.shard_map(
        local, mesh=split, in_specs=(cells, P(None, GX, None, "gz", None), P()), out_specs=cells, check_vma=False
    )
```

```python
import functools
import math

import jax
import jax.numpy as jnp
import numpy as np
from jax import lax
from jax.experimental import pallas as pl
from jax.experimental.pallas import tpu as pltpu
from jax.sharding import Mesh, PartitionSpec as P

SUB, LANE = 8, 128
EPS = 3e-6
F32, BF16 = jnp.float32, jnp.bfloat16


U1, U2 = 16, 4


def cell_flux(q, comp):
    r, m1, m2, m3, e, ev = q
    rinv = 1.0 / r
    kin = 0.5 * (m1 * m1 + m2 * m2 + m3 * m3) * rinv
    p = 0.4 * (e - kin - ev)
    un = q[comp] * rinv
    c = jnp.sqrt(1.4 * p * rinv)
    flux = [v * un for v in q]
    flux[comp] = flux[comp] + p
    flux[4] = (e + p) * un
    return flux, jnp.abs(un) + c


def correction(gmm, gm, gp, gpp):
    u0 = gmm - 1.375 * gm
    u1 = gm - 0.625 * gp
    u1r = gp - 0.625 * gm
    u2 = gpp - 1.375 * gp
    tm = (0.609375 * gm) * gm + EPS
    tp = (0.609375 * gp) * gp + EPS
    s0 = u0 * u0 + tm
    s1 = u1 * u1 + tp
    s2 = u2 * u2 + tp
    left = u0 + u1r
    right = u2 + u1
    p12 = s1 * s2
    p01 = s0 * s1
    p02 = s0 * s2
    w0 = p12 * p12
    w2 = 3.0 * (p01 * p01)
    w1 = 6.0 * (p02 * p02)
    num = (w0 + w0) * left + w2 * right
    den = w0 + w1 + w2
    return num * pl.reciprocal(den, approx=True)


def sweep(comp, cells, low, mid, high, put, gf_ref, gq_ref, mx_ref):
    def step(j, carry, q):
        flux, s = cell_flux(q, comp)
        pf, pq, ps = carry
        for v in range(6):
            gf_ref[v, j - 1] = flux[v] - pf[v]
            gq_ref[v, j - 1] = q[v] - pq[v]
        mx_ref[j - 1] = jnp.maximum(s, ps)
        return flux, q, s

    q0 = low(0)
    f0, s0 = cell_flux(q0, comp)
    carry = (f0, q0, s0)
    for j in (1, 2):
        carry = step(j, carry, low(j))
    carry = lax.fori_loop(0, cells, lambda j, c: step(j + 3, c, mid(j)), carry, unroll=U1)
    for j in range(3):
        carry = step(cells + 3 + j, carry, high(j))

    def face(f):
        a = jnp.maximum(jnp.maximum(mx_ref[f], mx_ref[f + 2]), mx_ref[f + 4])
        out = []
        for v in range(6):
            g = [gf_ref[v, f + k] for k in range(5)]
            h = [a * gq_ref[v, f + k] for k in range(5)]
            up = correction(g[0] + h[0], g[1] + h[1], g[2] + h[2], g[3] + h[3])
            down = correction(g[4] - h[4], g[3] - h[3], g[2] - h[2], g[1] - h[1])
            out.append((h[1] + h[3] - (h[2] + h[2])) + (down - up))
        return out

    def body(f, before):
        after = face(f)
        total = []
        for v in range(6):
            g = [gf_ref[v, f + k] for k in range(4)]
            total.append(7.0 * (g[2] + g[1]) - (g[3] + g[0]) + (after[v] - before[v]))
        put(f - 1, total)
        return after

    lax.fori_loop(1, cells + 1, body, face(0), unroll=U2)


def scratch(cells):
    return [
        pltpu.VMEM((6, cells + 5, SUB, LANE), F32),
        pltpu.VMEM((6, cells + 5, SUB, LANE), F32),
        pltpu.VMEM((cells + 5, SUB, LANE), F32),
    ]


def stream_kernel(flags, strength, q_ref, lo_ref, hi_ref, acc_in, out_ref, gf, gq, mx):
    nx = q_ref.shape[1]

    def mid(j):
        return [q_ref[v, j] for v in range(6)]

    def side(ref, flag, edge):
        def load(j):
            return [jnp.where(flag == 1, e, ref[v, j]) for v, e in enumerate(mid(edge))]
        return load

    def put(c, total):
        q = mid(c)
        rinv = 1.0 / q[0]
        p = 0.4 * (q[4] - 0.5 * (q[1] * q[1] + q[2] * q[2] + q[3] * q[3]) * rinv - q[5])
        temp = p * rinv
        share = 2.0 / (jnp.exp(2.0 / temp) - 1.0)
        lag = jnp.exp(1.5 * (jnp.exp(-jnp.log(temp) / 3.0) - 1.0))
        relax = (q[0] * share - q[5]) * (2.0 * p) / lag
        keep = 1.0 - 0.05 * strength[c]
        for v in range(6):
            new = keep * q[v] - (0.05 / 12.0) * (acc_in[v, c] + total[v])
            out_ref[v, c] = new + 0.05 * relax if v == 5 else new

    sweep(1, nx, side(lo_ref, flags[0], 0), mid, side(hi_ref, flags[1], nx - 1), put, gf, gq, mx)


def span_kernel(nz, q_ref, lo_ref, hi_ref, acc_in, acc_ref, gf, gq, mx):
    def rows(j):
        return pl.ds(j, SUB, stride=nz)

    def mid(j):
        return [q_ref[v, rows(j), :] for v in range(6)]

    def side(ref):
        return lambda j: [ref[j, v] for v in range(6)]

    def put(c, total):
        for v in range(6):
            acc_ref[v, rows(c), :] = acc_in[v, rows(c), :] + total[v]

    sweep(3, nz, side(lo_ref), mid, side(hi_ref), put, gf, gq, mx)


def wall_kernel(after, q_ref, out_ref, yq, yt, gf, gq, mx):
    ny = q_ref.shape[2]
    seg = ny // SUB
    for v in range(6):
        yq[v, SUB : SUB + ny] = q_ref[v].T
    q = [yq[v, SUB : 2 * SUB] for v in range(6)]
    rinv = 1.0 / q[0]
    temp = 0.4 * (q[4] - 0.5 * (q[1] * q[1] + q[2] * q[2] + q[3] * q[3]) * rinv - q[5]) * rinv
    ghost = [q[0], -q[1], -q[2], -q[3], q[4] - 2.5 * q[0] * (temp - 0.36 / temp), q[5]]
    for v in range(6):
        top = yq[v, SUB + ny - 1 : SUB + ny]
        for j in range(3):
            yq[v, SUB - 1 - j : SUB - j] = ghost[v][j : j + 1]
            yq[v, SUB + ny + j : SUB + ny + j + 1] = top

    def load(j):
        return [yq[v, pl.ds(SUB + j, SUB, stride=seg), :] for v in range(6)]

    def put(c, total):
        for v in range(6):
            yt[v, pl.ds(c, SUB, stride=seg), :] = total[v]

    sweep(2, seg, lambda j: load(j - 3), load, lambda j: load(seg + j), put, gf, gq, mx)

    for v in range(6):
        out_ref[v] = yt[v].T


def far(x):
    return pltpu.with_memory_space_constraint(x, pltpu.HBM)


def call(kernel, name, q, grid, in_specs, out_spec, shapes):
    return pl.pallas_call(
        kernel, out_shape=pltpu.HBM(q.shape, F32), name=name, grid=(grid,), in_specs=in_specs, out_specs=out_spec,
        scratch_shapes=shapes, compiler_params=pltpu.CompilerParams(vmem_limit_bytes=16 * 2**20),
        cost_estimate=pl.CostEstimate(flops=q.size * 700, bytes_accessed=q.size * 8, transcendentals=q.size * 2),
    )


SCALARS = pl.BlockSpec(memory_space=pltpu.SMEM)


def wall_sweep(q, after):
    _, nx, nz, ny = q.shape
    flat = q.reshape(6, nx * nz, ny)
    cells = pl.BlockSpec((6, LANE, ny), lambda t: (0, t, 0))
    shapes = [pltpu.VMEM((6, ny + 2 * SUB, LANE), F32), pltpu.VMEM((6, ny, LANE), F32)] + scratch(ny // SUB)
    return call(wall_kernel, "wall_sweep", flat, nx * nz // LANE, [SCALARS, cells], cells, shapes)(
        after, far(flat)).reshape(q.shape)


def span_sweep(q, zlo, zhi, acc):
    _, nx, nz, ny = q.shape
    flat = q.reshape(6, nx * nz, ny)
    cells = pl.BlockSpec((6, SUB * nz, ny), lambda t: (0, t, 0))
    side = pl.BlockSpec((3, 6, SUB, ny), lambda t: (0, 0, t, 0))
    return call(functools.partial(span_kernel, nz), "span_sweep", flat, nx // SUB, [cells, side, side, cells], cells, scratch(nz))(
        far(flat), zlo, zhi, far(acc.reshape(flat.shape))).reshape(q.shape)


def stream_sweep(q, xlo, xhi, acc, edges, strength):
    _, nx, nz, ny = q.shape
    cells = pl.BlockSpec((6, nx, SUB, ny), lambda t: (0, 0, t, 0))
    side = pl.BlockSpec((6, 3, SUB, ny), lambda t: (0, 0, t, 0))
    return call(stream_kernel, "stream_sweep", q, nz // SUB, [SCALARS, SCALARS, cells, side, side, cells], cells, scratch(nx))(
        edges, strength, far(q), xlo, xhi, far(acc))


def span_tables(modes, points):
    ids = np.arange(modes)[:, None] * np.arange(points)[None, :] % modes
    angle = 2.0 * np.pi / modes * ids
    cz, sz = np.cos(angle), np.sin(angle)
    return jnp.asarray(np.concatenate([np.concatenate([cz, sz], 1), np.concatenate([-sz, cz], 1)], 0), F32).astype(BF16)


def feed_kernel(first, count, chunk, depth, rows, stream_points, scalars, z_far, coeff_ref, out_ref, z_ref, buf, left_ref, rhs_a, rhs_b, acc_ref, sems):
    _, modes_x, _, levels, modes = coeff_ref.shape
    groups = levels // SUB
    points = z_far.shape[1] // 2
    steps = modes_x // chunk
    total = count * steps
    width = chunk * SUB
    sub = min(8, chunk)

    def copies(n, slot):
        k, v = lax.rem(n, steps) * chunk, first + lax.div(n, steps)
        return [
            pltpu.make_async_copy(coeff_ref.at[c, pl.ds(k, chunk), v], buf.at[slot, c], sems.at[slot, c]) for c in range(2)
        ]

    table = pltpu.make_async_copy(z_far, z_ref, sems.at[depth, 0])
    table.start()
    for n in range(min(depth - 1, total)):
        for copy in copies(n, n):
            copy.start()

    plane = lax.broadcasted_iota(jnp.int32, (rows, width), 0)
    mode = scalars[0] + lax.broadcasted_iota(jnp.int32, (rows, width), 1) // SUB
    station = jnp.zeros((rows, width), jnp.int32)
    for f in range(scalars.shape[0] - 1):
        station = jnp.where(plane == f, scalars[1 + f], station)
    own = lax.broadcasted_iota(jnp.int32, (rows, SUB, width), 2) % SUB == lax.broadcasted_iota(
        jnp.int32, (rows, SUB, width), 1
    )
    for k in range(steps):
        angle = (2.0 * math.pi / stream_points) * ((station * (mode + k * chunk)) % stream_points).astype(F32)
        for c, factor in enumerate((jnp.cos(angle), -jnp.sin(angle))):
            spread = jnp.where(own, factor[:, None, :], 0.0)
            left_ref[k, :, c * width : (c + 1) * width] = spread.reshape(rows * SUB, width).astype(BF16)

    def fetch(n):
        slot = lax.rem(n, depth)
        ahead = n + depth - 1

        @pl.when(ahead < total)
        def _():
            for copy in copies(ahead, lax.rem(ahead, depth)):
                copy.start()

        for copy in copies(n, slot):
            copy.wait()
        return slot

    def span(slot, rhs_ref):
        for i in range(0, chunk, sub):
            both = jnp.concatenate([buf[slot, c, i : i + sub].reshape(sub * levels, modes) for c in range(2)], axis=1)
            prod = jnp.dot(both, z_ref[...], preferred_element_type=F32).reshape(sub, groups, SUB, 2 * points)
            for g in range(groups):
                part = prod[:, g].reshape(sub * SUB, 2 * points).astype(BF16)
                for c in range(2):
                    row = c * width + i * SUB
                    rhs_ref[row : row + sub * SUB, g * points : (g + 1) * points] = part[:, c * points : (c + 1) * points]

    def stream(n, rhs_ref):
        k = lax.rem(n, steps)
        term = jnp.dot(left_ref[k], rhs_ref[...], preferred_element_type=F32)
        acc_ref[...] = jnp.where(k == 0, 0.0, acc_ref[...]) + term

    def give(n):
        @pl.when(lax.rem(n, steps) == steps - 1)
        def _():
            v = lax.div(n, steps)
            per = LANE // levels
            blocks, parts = out_ref.shape[:2]
            piece = points // parts
            short = piece // blocks
            for t in range(rows // per):
                tile = jnp.concatenate(
                    [
                        acc_ref[f * SUB : (f + 1) * SUB, g * points : (g + 1) * points]
                        for f in range(t * per, (t + 1) * per)
                        for g in range(groups)
                    ],
                    axis=0,
                )
                turned = tile.T
                for s in range(parts):
                    for b in range(blocks):
                        low = s * piece + b * short
                        out_ref[b, s, v, t] = turned[low : low + short]

    def both_stages(n, fill, drain):
        slot = fetch(n)
        stream(n - 1, drain)
        span(slot, fill)
        give(n - 1)

    table.wait()
    span(fetch(0), rhs_a)

    @pl.loop(0, (total - 1) // 2)
    def _(m):
        both_stages(2 * m + 1, rhs_b, rhs_a)
        both_stages(2 * m + 2, rhs_a, rhs_b)

    last = rhs_a
    if total % 2 == 0:
        both_stages(total - 1, rhs_b, rhs_a)
        last = rhs_b
    stream(total - 1, last)
    give(total - 1)


def feed(coeff, scalars, rows, stream_points, table, first, count, blocks, parts, chunk, depth):
    _, modes_x, _, levels, modes = coeff.shape
    points = table.shape[1] // 2
    groups = levels // SUB
    tiles = rows * levels // LANE
    chunk = min(chunk, modes_x)
    steps = modes_x // chunk
    flops = 2 * count * modes_x * levels * (2 * modes * 2 * points + rows * SUB * 2 * points)
    vmem = pl.BlockSpec(memory_space=pltpu.VMEM)
    return pl.pallas_call(
        functools.partial(feed_kernel, first, count, chunk, depth, rows, stream_points), name="feed",
        out_shape=jax.ShapeDtypeStruct((blocks, parts, count, tiles, points // parts // blocks, LANE), F32),
        in_specs=[SCALARS, pl.BlockSpec(memory_space=pl.ANY), pl.BlockSpec(memory_space=pl.ANY)], out_specs=vmem,
        scratch_shapes=[
            pltpu.VMEM(table.shape, BF16),
            pltpu.VMEM((depth, 2, chunk, levels, modes), BF16),
            pltpu.VMEM((steps, rows * SUB, 2 * chunk * SUB), BF16),
            pltpu.VMEM((2 * chunk * SUB, groups * points), BF16),
            pltpu.VMEM((2 * chunk * SUB, groups * points), BF16),
            pltpu.VMEM((rows * SUB, groups * points), F32),
            pltpu.SemaphoreType.DMA((depth + 1, 2)),
        ],
        compiler_params=pltpu.CompilerParams(vmem_limit_bytes=24 * 2**20),
        cost_estimate=pl.CostEstimate(flops=flops, bytes_accessed=2 * count * modes_x * levels * modes * 2, transcendentals=0),
    )(scalars, far(table), coeff)


def force_kernel(steps, per, levels, owners, offset, strength, *refs):
    far, state, out_ref = refs[:owners], refs[owners], refs[owners + 1]
    near, cells, sems = refs[owners + 2 : 2 * owners + 2], refs[-2], refs[-1]
    parts, variables, tiles, short, _ = near[0].shape

    def planes(t):
        return pl.ds(t * per, per)

    loads = [pltpu.make_async_copy(far[b], near[b], sems.at[b]) for b in range(owners)]
    reads = [pltpu.make_async_copy(state.at[:, planes(t)], cells.at[:, planes(t)], sems.at[owners + t]) for t in range(steps)]
    writes = [
        pltpu.make_async_copy(cells.at[:, planes(t)], out_ref.at[:, planes(t)], sems.at[owners + steps + t])
        for t in range(steps)
    ]
    for copy in loads + reads:
        copy.start()
    for copy in loads:
        copy.wait()
    lane = lax.broadcasted_iota(jnp.int32, (short, LANE), 1)
    for t in range(steps):
        reads[t].wait()
        tile = jnp.minimum(t + offset[0], tiles - 1)

        for v in range(variables):
            for b in range(owners):
                blocks = [near[b][s, v, tile] for s in range(parts)]
                for i in range(per):
                    row = blocks[0] if i == 0 else pltpu.roll(blocks[0], (-i * levels) % LANE, 1)
                    for s in range(1, parts):
                        moved = blocks[s] if s == i else pltpu.roll(blocks[s], ((s - i) * levels) % LANE, 1)
                        row = jnp.where(lane >= s * levels, moved, row)
                    some = pl.ds(b * short, short)
                    cells[v, t * per + i, some] = cells[v, t * per + i, some] + (0.05 * strength[t * per + i]) * row

        writes[t].start()
    for copy in writes:
        copy.wait()


def force(state, targets, strength, offset, levels, planes):
    variables, nx, nz, ny = state.shape
    per = LANE // levels
    steps = -(-min(planes, nx) // per)
    owners = len(targets)
    anywhere = pl.BlockSpec(memory_space=pl.ANY)
    return pl.pallas_call(
        functools.partial(force_kernel, steps, per, levels, owners), name="force",
        out_shape=jax.ShapeDtypeStruct(state.shape, F32),
        in_specs=[SCALARS, SCALARS] + [anywhere] * (owners + 1), out_specs=anywhere,
        scratch_shapes=[pltpu.VMEM(t.shape, F32) for t in targets]
        + [pltpu.VMEM((variables, steps * per, nz, ny), F32), pltpu.SemaphoreType.DMA((owners + 2 * steps,))],
        input_output_aliases={2 + owners: 0},
        compiler_params=pltpu.CompilerParams(vmem_limit_bytes=16 * 2**20),
    )(offset, strength, *targets, state)


GX = ("gh", "gl")


def local(state, coeff, feed_plane):
    high, low, parts = lax.axis_size("gh"), lax.axis_size("gl"), lax.axis_size("gz")
    gx = high * low
    me = lax.axis_index("gh") * low + lax.axis_index("gl")
    variables, nx, nz, ny = state.shape
    _, modes_x, _, levels, modes = coeff.shape
    planes = feed_plane.shape[0]

    per = LANE // levels
    rows = -(-planes // per) * per
    scalars = jnp.concatenate([jnp.reshape(me * modes_x, (1,)), feed_plane])
    ring = [(i, (i + 1) % parts) for i in range(parts)]
    line = [(i, i + 1) for i in range(gx - 1)]
    table = span_tables(modes, nz * parts)
    edges = jnp.stack([me == 0, me == gx - 1]).astype(jnp.int32)
    plane = me * nx + jnp.arange(nx, dtype=jnp.int32)
    strength = jnp.where(plane < planes, 2.0 * jnp.square(1.0 - plane.astype(F32) / planes), 0.0)

    def spread(part):
        part = part.reshape(-1, *part.shape[2:])
        part = lax.all_to_all(part, ("gl", "gz"), split_axis=0, concat_axis=0, tiled=True)
        return part.reshape(low, parts, *part.shape[1:]).sum(0)

    def gather(part):
        stride = 1
        while stride < high:
            hops = [(i, i - stride) for i in range(stride, high, 2 * stride)]
            part = part + lax.ppermute(part, "gh", hops)
            stride *= 2
        return part

    part = feed(coeff, scalars, rows, 2 * modes_x * gx, table, 0, variables, low, parts, 64, 3)
    part, edges, late = lax.optimization_barrier((part, edges, state))
    slabs = [late[:, nx - 3 :], late[:, :3]] + [jnp.stack([late[:, :, k + j] for j in range(3)]) for k in (nz - 3, 0)]
    part = spread(part)
    zlo = lax.ppermute(slabs[2], "gz", ring)
    zhi = lax.ppermute(slabs[3], "gz", [(j, i) for i, j in ring])
    acc = wall_sweep(state, edges)
    part, acc, zlo, zhi, *slabs = lax.optimization_barrier((part, acc, zlo, zhi, *slabs[:2]))
    xlo = lax.ppermute(slabs[0], GX, line)
    xhi = lax.ppermute(slabs[1], GX, [(j, i) for i, j in line])
    part = gather(part)
    acc = span_sweep(state, zlo, zhi, acc)
    part, acc = lax.optimization_barrier((part, acc))
    owned = [part] + [lax.ppermute(part, GX, [(i, 0)]) for i in range(1, low)]
    new = stream_sweep(state, xlo, xhi, acc, edges, strength)
    for other in range(1, -(-planes // nx)):
        owned = [jnp.where(me == other, lax.ppermute(t, GX, [(0, other)]), t) for t in owned]
    offset = jnp.reshape(me * nx // per, (1,))
    return force(new, owned, strength, offset, levels, planes)


def solution(mesh):
    gx, gz = mesh.devices.shape
    low = next(n for n in (4, 2, 1) if gx % n == 0)
    split = Mesh(mesh.devices.reshape(gx // low, low, gz), ("gh", "gl", "gz"))
    cells = P(None, GX, "gz", None)
    return jax.shard_map(
        local, mesh=split, in_specs=(cells, P(None, GX, None, "gz", None), P()), out_specs=cells, check_vma=False
    )
```

```python
import functools
import math

import jax
import jax.numpy as jnp
import numpy as np
from jax import lax
from jax.experimental import pallas as pl
from jax.experimental.pallas import tpu as pltpu
from jax.sharding import Mesh, PartitionSpec as P

SUB, LANE = 8, 128
EPS = 3e-6
F32, BF16 = jnp.float32, jnp.bfloat16


U1, U2 = 16, 4


def cell_flux(q, comp):
    r, m1, m2, m3, e, ev = q
    rinv = 1.0 / r
    kin = 0.5 * (m1 * m1 + m2 * m2 + m3 * m3) * rinv
    p = 0.4 * (e - kin - ev)
    un = q[comp] * rinv
    c = jnp.sqrt(1.4 * p * rinv)
    flux = [v * un for v in q]
    flux[comp] = flux[comp] + p
    flux[4] = (e + p) * un
    return flux, jnp.abs(un) + c


def correction(gmm, gm, gp, gpp):
    u0 = gmm - 1.375 * gm
    u1 = gm - 0.625 * gp
    u1r = gp - 0.625 * gm
    u2 = gpp - 1.375 * gp
    tm = (0.609375 * gm) * gm + EPS
    tp = (0.609375 * gp) * gp + EPS
    s0 = u0 * u0 + tm
    s1 = u1 * u1 + tp
    s2 = u2 * u2 + tp
    left = u0 + u1r
    right = u2 + u1
    p12 = s1 * s2
    p01 = s0 * s1
    p02 = s0 * s2
    w0 = p12 * p12
    w2 = 3.0 * (p01 * p01)
    w1 = 6.0 * (p02 * p02)
    num = (w0 + w0) * left + w2 * right
    den = w0 + w1 + w2
    return num * pl.reciprocal(den, approx=True)


def sweep(comp, cells, low, mid, high, put, gf_ref, gq_ref, mx_ref):
    def step(j, carry, q):
        flux, s = cell_flux(q, comp)
        pf, pq, ps = carry
        for v in range(6):
            gf_ref[v, j - 1] = flux[v] - pf[v]
            gq_ref[v, j - 1] = q[v] - pq[v]
        mx_ref[j - 1] = jnp.maximum(s, ps)
        return flux, q, s

    q0 = low(0)
    f0, s0 = cell_flux(q0, comp)
    carry = (f0, q0, s0)
    for j in (1, 2):
        carry = step(j, carry, low(j))
    carry = lax.fori_loop(0, cells, lambda j, c: step(j + 3, c, mid(j)), carry, unroll=U1)
    for j in range(3):
        carry = step(cells + 3 + j, carry, high(j))

    def face(f):
        a = jnp.maximum(jnp.maximum(mx_ref[f], mx_ref[f + 2]), mx_ref[f + 4])
        out = []
        for v in range(6):
            g = [gf_ref[v, f + k] for k in range(5)]
            h = [a * gq_ref[v, f + k] for k in range(5)]
            up = correction(g[0] + h[0], g[1] + h[1], g[2] + h[2], g[3] + h[3])
            down = correction(g[4] - h[4], g[3] - h[3], g[2] - h[2], g[1] - h[1])
            out.append((h[1] + h[3] - (h[2] + h[2])) + (down - up))
        return out

    def body(f, before):
        after = face(f)
        total = []
        for v in range(6):
            g = [gf_ref[v, f + k] for k in range(4)]
            total.append(7.0 * (g[2] + g[1]) - (g[3] + g[0]) + (after[v] - before[v]))
        put(f - 1, total)
        return after

    lax.fori_loop(1, cells + 1, body, face(0), unroll=U2)


def scratch(cells):
    return [
        pltpu.VMEM((6, cells + 5, SUB, LANE), F32),
        pltpu.VMEM((6, cells + 5, SUB, LANE), F32),
        pltpu.VMEM((cells + 5, SUB, LANE), F32),
    ]


def stream_kernel(flags, strength, q_ref, lo_ref, hi_ref, acc_in, out_ref, gf, gq, mx):
    nx = q_ref.shape[1]

    def mid(j):
        return [q_ref[v, j] for v in range(6)]

    def side(ref, flag, edge):
        def load(j):
            return [jnp.where(flag == 1, e, ref[v, j]) for v, e in enumerate(mid(edge))]
        return load

    def put(c, total):
        q = mid(c)
        rinv = 1.0 / q[0]
        p = 0.4 * (q[4] - 0.5 * (q[1] * q[1] + q[2] * q[2] + q[3] * q[3]) * rinv - q[5])
        temp = p * rinv
        share = 2.0 / (jnp.exp(2.0 / temp) - 1.0)
        lag = jnp.exp(1.5 * (jnp.exp(-jnp.log(temp) / 3.0) - 1.0))
        relax = (q[0] * share - q[5]) * (2.0 * p) / lag
        keep = 1.0 - 0.05 * strength[c]
        for v in range(6):
            new = keep * q[v] - (0.05 / 12.0) * (acc_in[v, c] + total[v])
            out_ref[v, c] = new + 0.05 * relax if v == 5 else new

    sweep(1, nx, side(lo_ref, flags[0], 0), mid, side(hi_ref, flags[1], nx - 1), put, gf, gq, mx)


def span_kernel(nz, q_ref, lo_ref, hi_ref, acc_in, acc_ref, gf, gq, mx):
    def rows(j):
        return pl.ds(j, SUB, stride=nz)

    def mid(j):
        return [q_ref[v, rows(j), :] for v in range(6)]

    def side(ref):
        return lambda j: [ref[j, v] for v in range(6)]

    def put(c, total):
        for v in range(6):
            acc_ref[v, rows(c), :] = acc_in[v, rows(c), :] + total[v]

    sweep(3, nz, side(lo_ref), mid, side(hi_ref), put, gf, gq, mx)


def wall_kernel(after, q_ref, out_ref, yq, yt, gf, gq, mx):
    ny = q_ref.shape[2]
    seg = ny // SUB
    for v in range(6):
        yq[v, SUB : SUB + ny] = q_ref[v].T
    q = [yq[v, SUB : 2 * SUB] for v in range(6)]
    rinv = 1.0 / q[0]
    temp = 0.4 * (q[4] - 0.5 * (q[1] * q[1] + q[2] * q[2] + q[3] * q[3]) * rinv - q[5]) * rinv
    ghost = [q[0], -q[1], -q[2], -q[3], q[4] - 2.5 * q[0] * (temp - 0.36 / temp), q[5]]
    for v in range(6):
        top = yq[v, SUB + ny - 1 : SUB + ny]
        for j in range(3):
            yq[v, SUB - 1 - j : SUB - j] = ghost[v][j : j + 1]
            yq[v, SUB + ny + j : SUB + ny + j + 1] = top

    def load(j):
        return [yq[v, pl.ds(SUB + j, SUB, stride=seg), :] for v in range(6)]

    def put(c, total):
        for v in range(6):
            yt[v, pl.ds(c, SUB, stride=seg), :] = total[v]

    sweep(2, seg, lambda j: load(j - 3), load, lambda j: load(seg + j), put, gf, gq, mx)

    for v in range(6):
        out_ref[v] = yt[v].T


def far(x):
    return pltpu.with_memory_space_constraint(x, pltpu.HBM)


def call(kernel, name, q, grid, in_specs, out_spec, shapes, place=pltpu.HBM):
    return pl.pallas_call(
        kernel, out_shape=place(q.shape, F32), name=name, grid=(grid,), in_specs=in_specs, out_specs=out_spec,
        scratch_shapes=shapes, compiler_params=pltpu.CompilerParams(vmem_limit_bytes=16 * 2**20),
        cost_estimate=pl.CostEstimate(flops=q.size * 700, bytes_accessed=q.size * 8, transcendentals=q.size * 2),
    )


SCALARS = pl.BlockSpec(memory_space=pltpu.SMEM)


def wall_sweep(q, after):
    _, nx, nz, ny = q.shape
    flat = q.reshape(6, nx * nz, ny)
    cells = pl.BlockSpec((6, LANE, ny), lambda t: (0, t, 0))
    shapes = [pltpu.VMEM((6, ny + 2 * SUB, LANE), F32), pltpu.VMEM((6, ny, LANE), F32)] + scratch(ny // SUB)
    return call(wall_kernel, "wall_sweep", flat, nx * nz // LANE, [SCALARS, cells], cells, shapes)(
        after, far(flat)).reshape(q.shape)


def span_sweep(q, zlo, zhi, acc):
    _, nx, nz, ny = q.shape
    flat = q.reshape(6, nx * nz, ny)
    cells = pl.BlockSpec((6, SUB * nz, ny), lambda t: (0, t, 0))
    side = pl.BlockSpec((3, 6, SUB, ny), lambda t: (0, 0, t, 0))
    return call(functools.partial(span_kernel, nz), "span_sweep", flat, nx // SUB, [cells, side, side, cells], cells, scratch(nz))(
        far(flat), zlo, zhi, far(acc.reshape(flat.shape))).reshape(q.shape)


def stream_sweep(q, xlo, xhi, acc, edges, strength):
    _, nx, nz, ny = q.shape
    cells = pl.BlockSpec((6, nx, SUB, ny), lambda t: (0, 0, t, 0))
    side = pl.BlockSpec((6, 3, SUB, ny), lambda t: (0, 0, t, 0))
    return call(stream_kernel, "stream_sweep", q, nz // SUB, [SCALARS, SCALARS, cells, side, side, cells], cells, scratch(nx), pltpu.VMEM)(
        edges, strength, far(q), xlo, xhi, far(acc))


BIT = 32


def span_tables(modes, points):
    ids = np.arange(modes)[:, None] * np.arange(points)[None, :] % modes
    angle = 2.0 * np.pi / modes * ids
    cz, sz = np.cos(angle), np.sin(angle)
    return jnp.asarray(np.concatenate([np.concatenate([cz, sz], 1), np.concatenate([-sz, cz], 1)], 0), F32).astype(BF16)


def feed_kernel(first, count, chunk, depth, rows, stream_points, base, stations, z_far, coeff_ref, out_ref, z_ref, buf, left_ref, rhs_a, rhs_b, acc_ref, sems):
    _, modes_x, _, levels, modes = coeff_ref.shape
    groups = levels // SUB
    points = z_far.shape[1] // 2
    steps = modes_x // chunk
    total = count * steps
    width = chunk * SUB
    sub = min(8, chunk)
    bit = min(BIT, chunk)

    def copies(n, slot):
        k, v = lax.rem(n, steps) * chunk, first + lax.div(n, steps)
        return [
            pltpu.make_async_copy(coeff_ref.at[c, pl.ds(k, chunk), v], buf.at[slot, c], sems.at[slot, c]) for c in range(2)
        ]

    table = pltpu.make_async_copy(z_far, z_ref, sems.at[depth, 0])
    table.start()
    pieces = [
        [
            pltpu.make_async_copy(
                coeff_ref.at[c, i * bit : (i + 1) * bit, first], buf.at[0, c, i * bit : (i + 1) * bit], sems.at[depth + 1 + i, c]
            )
            for c in range(2)
        ]
        for i in range(chunk // bit)
    ]
    for pair in pieces:
        for copy in pair:
            copy.start()
    for n in range(1, min(depth, total)):
        for copy in copies(n, n):
            copy.start()

    def fetch(n):
        slot = lax.rem(n, depth)
        ahead = n + depth - 1

        @pl.when(ahead < total)
        def _():
            for copy in copies(ahead, lax.rem(ahead, depth)):
                copy.start()

        for copy in copies(n, slot):
            copy.wait()
        return slot

    def span(slot, rhs_ref, pieces=()):
        for i in range(0, chunk, sub):
            if pieces and i % bit == 0:
                for copy in pieces[i // bit]:
                    copy.wait()
            both = jnp.concatenate([buf[slot, c, i : i + sub].reshape(sub * levels, modes) for c in range(2)], axis=1)
            prod = jnp.dot(both, z_ref[...], preferred_element_type=F32).reshape(sub, groups, SUB, 2 * points)
            for g in range(groups):
                part = prod[:, g].reshape(sub * SUB, 2 * points).astype(BF16)
                for c in range(2):
                    row = c * width + i * SUB
                    rhs_ref[row : row + sub * SUB, g * points : (g + 1) * points] = part[:, c * points : (c + 1) * points]

    def stream(n, rhs_ref):
        k = lax.rem(n, steps)
        term = jnp.dot(left_ref[k], rhs_ref[...], preferred_element_type=F32)
        acc_ref[...] = jnp.where(k == 0, 0.0, acc_ref[...]) + term

    def give(n):
        @pl.when(lax.rem(n, steps) == steps - 1)
        def _():
            v = lax.div(n, steps)
            per = LANE // levels
            blocks, parts = out_ref.shape[:2]
            piece = points // parts
            short = piece // blocks
            for t in range(rows // per):
                tile = jnp.concatenate(
                    [
                        acc_ref[f * SUB : (f + 1) * SUB, g * points : (g + 1) * points]
                        for f in range(t * per, (t + 1) * per)
                        for g in range(groups)
                    ],
                    axis=0,
                )
                turned = tile.T
                for s in range(parts):
                    for b in range(blocks):
                        low = s * piece + b * short
                        out_ref[b, s, v, t] = turned[low : low + short]

    def both_stages(n, fill, drain):
        slot = fetch(n)
        stream(n - 1, drain)
        span(slot, fill)
        give(n - 1)

    table.wait()
    span(0, rhs_a, pieces)
    plane = lax.broadcasted_iota(jnp.int32, (rows, width), 0)
    mode = base[0] + lax.broadcasted_iota(jnp.int32, (rows, width), 1) // SUB
    station = jnp.zeros((rows, width), jnp.int32)
    for f in range(stations.shape[0]):
        station = jnp.where(plane == f, stations[f], station)
    own = lax.broadcasted_iota(jnp.int32, (rows, SUB, width), 2) % SUB == lax.broadcasted_iota(
        jnp.int32, (rows, SUB, width), 1
    )
    for k in range(steps):
        angle = (2.0 * math.pi / stream_points) * ((station * (mode + k * chunk)) % stream_points).astype(F32)
        for c, factor in enumerate((jnp.cos(angle), -jnp.sin(angle))):
            spread = jnp.where(own, factor[:, None, :], 0.0)
            left_ref[k, :, c * width : (c + 1) * width] = spread.reshape(rows * SUB, width).astype(BF16)

    @pl.loop(0, (total - 1) // 2)
    def _(m):
        both_stages(2 * m + 1, rhs_b, rhs_a)
        both_stages(2 * m + 2, rhs_a, rhs_b)

    last = rhs_a
    if total % 2 == 0:
        both_stages(total - 1, rhs_b, rhs_a)
        last = rhs_b
    stream(total - 1, last)
    give(total - 1)


def feed(coeff, base, stations, rows, stream_points, table, first, count, blocks, parts, chunk, depth):
    _, modes_x, _, levels, modes = coeff.shape
    points = table.shape[1] // 2
    groups = levels // SUB
    tiles = rows * levels // LANE
    chunk = min(chunk, modes_x)
    steps = modes_x // chunk
    flops = 2 * count * modes_x * levels * (2 * modes * 2 * points + rows * SUB * 2 * points)
    vmem = pl.BlockSpec(memory_space=pltpu.VMEM)
    return pl.pallas_call(
        functools.partial(feed_kernel, first, count, chunk, depth, rows, stream_points), name="feed",
        out_shape=jax.ShapeDtypeStruct((blocks, parts, count, tiles, points // parts // blocks, LANE), F32),
        in_specs=[SCALARS, SCALARS, pl.BlockSpec(memory_space=pl.ANY), pl.BlockSpec(memory_space=pl.ANY)], out_specs=vmem,
        scratch_shapes=[
            pltpu.VMEM(table.shape, BF16),
            pltpu.VMEM((depth, 2, chunk, levels, modes), BF16),
            pltpu.VMEM((steps, rows * SUB, 2 * chunk * SUB), BF16),
            pltpu.VMEM((2 * chunk * SUB, groups * points), BF16),
            pltpu.VMEM((2 * chunk * SUB, groups * points), BF16),
            pltpu.VMEM((rows * SUB, groups * points), F32),
            pltpu.SemaphoreType.DMA((depth + 1 + chunk // min(BIT, chunk), 2)),
        ],
        compiler_params=pltpu.CompilerParams(vmem_limit_bytes=24 * 2**20),
        cost_estimate=pl.CostEstimate(flops=flops, bytes_accessed=2 * count * modes_x * levels * modes * 2, transcendentals=0),
    )(base, stations, far(table), coeff)


def force_kernel(steps, per, levels, where, offset, strength, *refs):
    *near, state, out_ref, cells, sems = refs
    parts, _, tiles, short, _ = near[0].shape
    variables = state.shape[0]
    forced = steps * per
    copies = []
    if forced < state.shape[1]:
        copies.append(pltpu.make_async_copy(state.at[:, forced:], out_ref.at[:, forced:], sems.at[steps]))
        copies[0].start()
    lane = lax.broadcasted_iota(jnp.int32, (short, LANE), 1)
    for t in range(steps):
        tile = jnp.minimum(t + offset[0], tiles - 1)
        for v in range(variables):
            for b, places in enumerate(where):
                source, row = places[v]
                blocks = [near[source][s, row, tile] for s in range(parts)]
                for i in range(per):
                    row = blocks[0] if i == 0 else pltpu.roll(blocks[0], (-i * levels) % LANE, 1)
                    for s in range(1, parts):
                        moved = blocks[s] if s == i else pltpu.roll(blocks[s], ((s - i) * levels) % LANE, 1)
                        row = jnp.where(lane >= s * levels, moved, row)
                    some = pl.ds(b * short, short)
                    cells[v, t * per + i, some] = state[v, t * per + i, some] + (0.05 * strength[t * per + i]) * row
        planes = pl.ds(t * per, per)
        copies.append(pltpu.make_async_copy(cells.at[:, planes], out_ref.at[:, planes], sems.at[t]))
        copies[-1].start()
    for copy in copies:
        copy.wait()


def force(state, targets, where, strength, offset, levels, planes):
    variables, nx, nz, ny = state.shape
    per = LANE // levels
    steps = -(-min(planes, nx) // per)
    owners = len(targets)
    vmem = pl.BlockSpec(memory_space=pltpu.VMEM)
    return pl.pallas_call(
        functools.partial(force_kernel, steps, per, levels, where), name="force",
        out_shape=jax.ShapeDtypeStruct(state.shape, F32),
        in_specs=[SCALARS, SCALARS] + [vmem] * (owners + 1), out_specs=pl.BlockSpec(memory_space=pl.ANY),
        scratch_shapes=[pltpu.VMEM((variables, steps * per, nz, ny), F32), pltpu.SemaphoreType.DMA((steps + 1,))],
        compiler_params=pltpu.CompilerParams(vmem_limit_bytes=16 * 2**20),
    )(offset, strength, *targets, state)


GX = ("gh", "gl")


def local(state, coeff, feed_plane):
    high, low, parts = lax.axis_size("gh"), lax.axis_size("gl"), lax.axis_size("gz")
    gx = high * low
    me = lax.axis_index("gh") * low + lax.axis_index("gl")
    variables, nx, nz, ny = state.shape
    _, modes_x, _, levels, modes = coeff.shape
    planes = feed_plane.shape[0]

    per = LANE // levels
    rows = -(-planes // per) * per
    base = jnp.reshape(me * modes_x, (1,))
    ring = [(i, (i + 1) % parts) for i in range(parts)]
    line = [(i, i + 1) for i in range(gx - 1)]
    table = span_tables(modes, nz * parts)
    edges = jnp.stack([me == 0, me == gx - 1]).astype(jnp.int32)
    plane = me * nx + jnp.arange(nx, dtype=jnp.int32)
    strength = jnp.where(plane < planes, 2.0 * jnp.square(1.0 - plane.astype(F32) / planes), 0.0)

    def spread(part):
        part = part.reshape(-1, *part.shape[2:])
        part = lax.all_to_all(part, ("gl", "gz"), split_axis=0, concat_axis=0, tiled=True)
        return part.reshape(low, parts, *part.shape[1:]).sum(0)

    relay = low == 4 and high > 1 and high & (high - 1) == 0 and variables % 2 == 0
    half = variables // 2

    def gather(part):
        stride = 1
        while stride < (high // 2 if relay else high):
            hops = [(i, i - stride) for i in range(stride, high, 2 * stride)]
            part = part + lax.ppermute(part, "gh", hops)
            stride *= 2
        if not relay:
            return part
        top = stride * low
        upper = lax.axis_index("gh") == stride
        main = lax.ppermute(part, GX, [(top + i, i) for i in range(3)])
        left = lax.ppermute(jnp.where(upper, part[:, half:], part[:, :half]), GX, [(3, 1), (top + 3, 2)])
        right = lax.ppermute(jnp.where(upper, part[:, :half], part[:, half:]), GX, [(3, 2), (top + 3, 1)])
        return part + main, left + right

    part = feed(coeff, base, feed_plane, rows, 2 * modes_x * gx, table, 0, variables, low, parts, 64, 3)
    part, edges, late = lax.optimization_barrier((part, edges, state))
    slabs = [late[:, nx - 3 :], late[:, :3]] + [jnp.stack([late[:, :, k + j] for j in range(3)]) for k in (nz - 3, 0)]
    part = spread(part)
    zlo = lax.ppermute(slabs[2], "gz", ring)
    zhi = lax.ppermute(slabs[3], "gz", [(j, i) for i, j in ring])
    acc = wall_sweep(state, edges)
    part, acc, zlo, zhi, *slabs = lax.optimization_barrier((part, acc, zlo, zhi, *slabs[:2]))
    xlo = lax.ppermute(slabs[0], GX, line)
    xhi = lax.ppermute(slabs[1], GX, [(j, i) for i, j in line])
    part = gather(part)
    acc = span_sweep(state, zlo, zhi, acc)
    part, acc = lax.optimization_barrier((part, acc))
    if relay:
        part, extra = part
        owned = [part] + [lax.ppermute(t, GX, [(i, 0)]) for t in (part, extra) for i in (1, 2)]
    else:
        owned = [part] + [lax.ppermute(part, GX, [(i, 0)]) for i in range(1, low)]
    new = stream_sweep(state, xlo, xhi, acc, edges, strength)
    for other in range(1, -(-planes // nx)):
        owned = [jnp.where(me == other, lax.ppermute(t, GX, [(0, other)]), t) for t in owned]
    offset = jnp.reshape(me * nx // per, (1,))
    where = [[(b, v) for v in range(variables)] for b in range(low)]
    if relay:
        where[3] = [(3 + v // half, v % half) for v in range(variables)]
    return force(new, owned, where, strength, offset, levels, planes)


def solution(mesh):
    gx, gz = mesh.devices.shape
    low = next(n for n in (4, 2, 1) if gx % n == 0)
    split = Mesh(mesh.devices.reshape(gx // low, low, gz), ("gh", "gl", "gz"))
    cells = P(None, GX, "gz", None)
    return jax.shard_map(
        local, mesh=split, in_specs=(cells, P(None, GX, None, "gz", None), P()), out_specs=cells, check_vma=False
    )
```

```python
import functools
import math

import jax
import jax.numpy as jnp
import numpy as np
from jax import lax
from jax.experimental import pallas as pl
from jax.experimental.pallas import tpu as pltpu
from jax.sharding import Mesh, PartitionSpec as P

SUB, LANE = 8, 128
EPS = 3e-6
F32, BF16 = jnp.float32, jnp.bfloat16


U1, U2 = 16, 4


def cell_flux(q, comp):
    r, m1, m2, m3, e, ev = q
    rinv = 1.0 / r
    kin = 0.5 * (m1 * m1 + m2 * m2 + m3 * m3) * rinv
    p = 0.4 * (e - kin - ev)
    un = q[comp] * rinv
    c = jnp.sqrt(1.4 * p * rinv)
    flux = [v * un for v in q]
    flux[comp] = flux[comp] + p
    flux[4] = (e + p) * un
    return flux, jnp.abs(un) + c


def correction(gmm, gm, gp, gpp):
    u0 = gmm - 1.375 * gm
    u1 = gm - 0.625 * gp
    u1r = gp - 0.625 * gm
    u2 = gpp - 1.375 * gp
    tm = (0.609375 * gm) * gm + EPS
    tp = (0.609375 * gp) * gp + EPS
    s0 = u0 * u0 + tm
    s1 = u1 * u1 + tp
    s2 = u2 * u2 + tp
    left = u0 + u1r
    right = u2 + u1
    p12 = s1 * s2
    p01 = s0 * s1
    p02 = s0 * s2
    w0 = p12 * p12
    w2 = 3.0 * (p01 * p01)
    w1 = 6.0 * (p02 * p02)
    num = (w0 + w0) * left + w2 * right
    den = w0 + w1 + w2
    return num * pl.reciprocal(den, approx=True)


def sweep(comp, cells, low, mid, high, put, gf_ref, gq_ref, mx_ref):
    def step(j, carry, q):
        flux, s = cell_flux(q, comp)
        pf, pq, ps = carry
        for v in range(6):
            gf_ref[v, j - 1] = flux[v] - pf[v]
            gq_ref[v, j - 1] = q[v] - pq[v]
        mx_ref[j - 1] = jnp.maximum(s, ps)
        return flux, q, s

    q0 = low(0)
    f0, s0 = cell_flux(q0, comp)
    carry = (f0, q0, s0)
    for j in (1, 2):
        carry = step(j, carry, low(j))
    carry = lax.fori_loop(0, cells, lambda j, c: step(j + 3, c, mid(j)), carry, unroll=U1)
    for j in range(3):
        carry = step(cells + 3 + j, carry, high(j))

    def face(f):
        a = jnp.maximum(jnp.maximum(mx_ref[f], mx_ref[f + 2]), mx_ref[f + 4])
        out = []
        for v in range(6):
            g = [gf_ref[v, f + k] for k in range(5)]
            h = [a * gq_ref[v, f + k] for k in range(5)]
            up = correction(g[0] + h[0], g[1] + h[1], g[2] + h[2], g[3] + h[3])
            down = correction(g[4] - h[4], g[3] - h[3], g[2] - h[2], g[1] - h[1])
            out.append((h[1] + h[3] - (h[2] + h[2])) + (down - up))
        return out

    def body(f, before):
        after = face(f)
        total = []
        for v in range(6):
            g = [gf_ref[v, f + k] for k in range(4)]
            total.append(7.0 * (g[2] + g[1]) - (g[3] + g[0]) + (after[v] - before[v]))
        put(f - 1, total)
        return after

    lax.fori_loop(1, cells + 1, body, face(0), unroll=U2)


def scratch(cells):
    return [
        pltpu.VMEM((6, cells + 5, SUB, LANE), F32),
        pltpu.VMEM((6, cells + 5, SUB, LANE), F32),
        pltpu.VMEM((cells + 5, SUB, LANE), F32),
    ]


def stream_kernel(flags, strength, q_ref, lo_ref, hi_ref, wall, span, out_ref, gf, gq, mx):
    nx = q_ref.shape[1]

    def mid(j):
        return [q_ref[v, j] for v in range(6)]

    def side(ref, flag, edge):
        def load(j):
            return [jnp.where(flag == 1, e, ref[v, j]) for v, e in enumerate(mid(edge))]
        return load

    def put(c, total):
        q = mid(c)
        rinv = 1.0 / q[0]
        p = 0.4 * (q[4] - 0.5 * (q[1] * q[1] + q[2] * q[2] + q[3] * q[3]) * rinv - q[5])
        temp = p * rinv
        share = 2.0 / (jnp.exp(2.0 / temp) - 1.0)
        lag = jnp.exp(1.5 * (jnp.exp(-jnp.log(temp) / 3.0) - 1.0))
        relax = (q[0] * share - q[5]) * (2.0 * p) / lag
        keep = 1.0 - 0.05 * strength[c]
        for v in range(6):
            new = keep * q[v] - (0.05 / 12.0) * (wall[v, c] + span[v, c] + total[v])
            out_ref[v, c] = new + 0.05 * relax if v == 5 else new

    sweep(1, nx, side(lo_ref, flags[0], 0), mid, side(hi_ref, flags[1], nx - 1), put, gf, gq, mx)


def span_kernel(nz, q_ref, lo_ref, hi_ref, acc_ref, gf, gq, mx):
    def rows(j):
        return pl.ds(j, SUB, stride=nz)

    def mid(j):
        return [q_ref[v, rows(j), :] for v in range(6)]

    def side(ref):
        return lambda j: [ref[j, v] for v in range(6)]

    def put(c, total):
        for v in range(6):
            acc_ref[v, rows(c), :] = total[v]

    sweep(3, nz, side(lo_ref), mid, side(hi_ref), put, gf, gq, mx)


def wall_kernel(after, q_ref, out_ref, yq, yt, gf, gq, mx):
    ny = q_ref.shape[2]
    seg = ny // SUB
    for v in range(6):
        yq[v, SUB : SUB + ny] = q_ref[v].T
    q = [yq[v, SUB : 2 * SUB] for v in range(6)]
    rinv = 1.0 / q[0]
    temp = 0.4 * (q[4] - 0.5 * (q[1] * q[1] + q[2] * q[2] + q[3] * q[3]) * rinv - q[5]) * rinv
    ghost = [q[0], -q[1], -q[2], -q[3], q[4] - 2.5 * q[0] * (temp - 0.36 / temp), q[5]]
    for v in range(6):
        top = yq[v, SUB + ny - 1 : SUB + ny]
        for j in range(3):
            yq[v, SUB - 1 - j : SUB - j] = ghost[v][j : j + 1]
            yq[v, SUB + ny + j : SUB + ny + j + 1] = top

    def load(j):
        return [yq[v, pl.ds(SUB + j, SUB, stride=seg), :] for v in range(6)]

    def put(c, total):
        for v in range(6):
            yt[v, pl.ds(c, SUB, stride=seg), :] = total[v]

    sweep(2, seg, lambda j: load(j - 3), load, lambda j: load(seg + j), put, gf, gq, mx)

    for v in range(6):
        out_ref[v] = yt[v].T


def far(x):
    return pltpu.with_memory_space_constraint(x, pltpu.HBM)


def call(kernel, name, q, grid, in_specs, out_spec, shapes, place=pltpu.HBM):
    return pl.pallas_call(
        kernel, out_shape=place(q.shape, F32), name=name, grid=(grid,), in_specs=in_specs, out_specs=out_spec,
        scratch_shapes=shapes, compiler_params=pltpu.CompilerParams(vmem_limit_bytes=16 * 2**20),
        cost_estimate=pl.CostEstimate(flops=q.size * 700, bytes_accessed=q.size * 8, transcendentals=q.size * 2),
    )


SCALARS = pl.BlockSpec(memory_space=pltpu.SMEM)


def wall_sweep(q, after):
    _, nx, nz, ny = q.shape
    flat = q.reshape(6, nx * nz, ny)
    cells = pl.BlockSpec((6, LANE, ny), lambda t: (0, t, 0))
    shapes = [pltpu.VMEM((6, ny + 2 * SUB, LANE), F32), pltpu.VMEM((6, ny, LANE), F32)] + scratch(ny // SUB)
    return call(wall_kernel, "wall_sweep", flat, nx * nz // LANE, [SCALARS, cells], cells, shapes)(
        after, far(flat)).reshape(q.shape)


def span_sweep(q, zlo, zhi):
    _, nx, nz, ny = q.shape
    flat = q.reshape(6, nx * nz, ny)
    cells = pl.BlockSpec((6, SUB * nz, ny), lambda t: (0, t, 0))
    side = pl.BlockSpec((3, 6, SUB, ny), lambda t: (0, 0, t, 0))
    return call(functools.partial(span_kernel, nz), "span_sweep", flat, nx // SUB, [cells, side, side], cells, scratch(nz))(
        far(flat), zlo, zhi).reshape(q.shape)


def stream_sweep(q, xlo, xhi, wall, span, edges, strength):
    _, nx, nz, ny = q.shape
    cells = pl.BlockSpec((6, nx, SUB, ny), lambda t: (0, 0, t, 0))
    side = pl.BlockSpec((6, 3, SUB, ny), lambda t: (0, 0, t, 0))
    return call(stream_kernel, "stream_sweep", q, nz // SUB, [SCALARS, SCALARS, cells, side, side, cells, cells], cells, scratch(nx), pltpu.VMEM)(
        edges, strength, far(q), xlo, xhi, far(wall), far(span))


BIT = 32


def span_tables(modes, points):
    ids = np.arange(modes)[:, None] * np.arange(points)[None, :] % modes
    angle = 2.0 * np.pi / modes * ids
    cz, sz = np.cos(angle), np.sin(angle)
    return jnp.asarray(np.concatenate([np.concatenate([cz, sz], 1), np.concatenate([-sz, cz], 1)], 0), F32).astype(BF16)


def feed_kernel(first, count, chunk, depth, rows, stream_points, base, stations, z_far, coeff_ref, out_ref, z_ref, buf, left_ref, rhs_a, rhs_b, acc_ref, sems):
    _, modes_x, _, levels, modes = coeff_ref.shape
    groups = levels // SUB
    points = z_far.shape[1] // 2
    steps = modes_x // chunk
    total = count * steps
    width = chunk * SUB
    sub = min(8, chunk)
    bit = min(BIT, chunk)

    def copies(n, slot):
        k, v = lax.rem(n, steps) * chunk, first + lax.div(n, steps)
        return [
            pltpu.make_async_copy(coeff_ref.at[c, pl.ds(k, chunk), v], buf.at[slot, c], sems.at[slot, c]) for c in range(2)
        ]

    table = pltpu.make_async_copy(z_far, z_ref, sems.at[depth, 0])
    table.start()
    pieces = [
        [
            pltpu.make_async_copy(
                coeff_ref.at[c, i * bit : (i + 1) * bit, first], buf.at[0, c, i * bit : (i + 1) * bit], sems.at[depth + 1 + i, c]
            )
            for c in range(2)
        ]
        for i in range(chunk // bit)
    ]
    for pair in pieces:
        for copy in pair:
            copy.start()
    for n in range(1, min(depth, total)):
        for copy in copies(n, n):
            copy.start()

    def fetch(n):
        slot = lax.rem(n, depth)
        ahead = n + depth - 1

        @pl.when(ahead < total)
        def _():
            for copy in copies(ahead, lax.rem(ahead, depth)):
                copy.start()

        for copy in copies(n, slot):
            copy.wait()
        return slot

    def span(slot, rhs_ref, pieces=()):
        for i in range(0, chunk, sub):
            if pieces and i % bit == 0:
                for copy in pieces[i // bit]:
                    copy.wait()
            both = jnp.concatenate([buf[slot, c, i : i + sub].reshape(sub * levels, modes) for c in range(2)], axis=1)
            prod = jnp.dot(both, z_ref[...], preferred_element_type=F32).reshape(sub, groups, SUB, 2 * points)
            for g in range(groups):
                part = prod[:, g].reshape(sub * SUB, 2 * points).astype(BF16)
                for c in range(2):
                    row = c * width + i * SUB
                    rhs_ref[row : row + sub * SUB, g * points : (g + 1) * points] = part[:, c * points : (c + 1) * points]

    def stream(n, rhs_ref):
        k = lax.rem(n, steps)
        term = jnp.dot(left_ref[k], rhs_ref[...], preferred_element_type=F32)
        acc_ref[...] = jnp.where(k == 0, 0.0, acc_ref[...]) + term

    def give(n):
        @pl.when(lax.rem(n, steps) == steps - 1)
        def _():
            v = lax.div(n, steps)
            per = LANE // levels
            blocks, parts = out_ref.shape[:2]
            piece = points // parts
            short = piece // blocks
            for t in range(rows // per):
                tile = jnp.concatenate(
                    [
                        acc_ref[f * SUB : (f + 1) * SUB, g * points : (g + 1) * points]
                        for f in range(t * per, (t + 1) * per)
                        for g in range(groups)
                    ],
                    axis=0,
                )
                turned = tile.T
                for s in range(parts):
                    for b in range(blocks):
                        low = s * piece + b * short
                        out_ref[b, s, v, t] = turned[low : low + short]

    def both_stages(n, fill, drain):
        slot = fetch(n)
        stream(n - 1, drain)
        span(slot, fill)
        give(n - 1)

    table.wait()
    span(0, rhs_a, pieces)
    plane = lax.broadcasted_iota(jnp.int32, (rows, width), 0)
    mode = base[0] + lax.broadcasted_iota(jnp.int32, (rows, width), 1) // SUB
    station = jnp.zeros((rows, width), jnp.int32)
    for f in range(stations.shape[0]):
        station = jnp.where(plane == f, stations[f], station)
    own = lax.broadcasted_iota(jnp.int32, (rows, SUB, width), 2) % SUB == lax.broadcasted_iota(
        jnp.int32, (rows, SUB, width), 1
    )
    for k in range(steps):
        angle = (2.0 * math.pi / stream_points) * ((station * (mode + k * chunk)) % stream_points).astype(F32)
        for c, factor in enumerate((jnp.cos(angle), -jnp.sin(angle))):
            spread = jnp.where(own, factor[:, None, :], 0.0)
            left_ref[k, :, c * width : (c + 1) * width] = spread.reshape(rows * SUB, width).astype(BF16)

    @pl.loop(0, (total - 1) // 2)
    def _(m):
        both_stages(2 * m + 1, rhs_b, rhs_a)
        both_stages(2 * m + 2, rhs_a, rhs_b)

    last = rhs_a
    if total % 2 == 0:
        both_stages(total - 1, rhs_b, rhs_a)
        last = rhs_b
    stream(total - 1, last)
    give(total - 1)


def feed(coeff, base, stations, rows, stream_points, table, first, count, blocks, parts, chunk, depth):
    _, modes_x, _, levels, modes = coeff.shape
    points = table.shape[1] // 2
    groups = levels // SUB
    tiles = rows * levels // LANE
    chunk = min(chunk, modes_x)
    steps = modes_x // chunk
    flops = 2 * count * modes_x * levels * (2 * modes * 2 * points + rows * SUB * 2 * points)
    vmem = pl.BlockSpec(memory_space=pltpu.VMEM)
    return pl.pallas_call(
        functools.partial(feed_kernel, first, count, chunk, depth, rows, stream_points), name="feed",
        out_shape=jax.ShapeDtypeStruct((blocks, parts, count, tiles, points // parts // blocks, LANE), F32),
        in_specs=[SCALARS, SCALARS, pl.BlockSpec(memory_space=pl.ANY), pl.BlockSpec(memory_space=pl.ANY)], out_specs=vmem,
        scratch_shapes=[
            pltpu.VMEM(table.shape, BF16),
            pltpu.VMEM((depth, 2, chunk, levels, modes), BF16),
            pltpu.VMEM((steps, rows * SUB, 2 * chunk * SUB), BF16),
            pltpu.VMEM((2 * chunk * SUB, groups * points), BF16),
            pltpu.VMEM((2 * chunk * SUB, groups * points), BF16),
            pltpu.VMEM((rows * SUB, groups * points), F32),
            pltpu.SemaphoreType.DMA((depth + 1 + chunk // min(BIT, chunk), 2)),
        ],
        compiler_params=pltpu.CompilerParams(vmem_limit_bytes=24 * 2**20),
        cost_estimate=pl.CostEstimate(flops=flops, bytes_accessed=2 * count * modes_x * levels * modes * 2, transcendentals=0),
    )(base, stations, far(table), coeff)


def force_kernel(steps, per, levels, where, offset, strength, *refs):
    *near, state, out_ref, cells, sems = refs
    parts, _, tiles, short, _ = near[0].shape
    variables = state.shape[0]
    forced = steps * per
    copies = []
    if forced < state.shape[1]:
        copies.append(pltpu.make_async_copy(state.at[:, forced:], out_ref.at[:, forced:], sems.at[steps]))
        copies[0].start()
    lane = lax.broadcasted_iota(jnp.int32, (short, LANE), 1)
    for t in range(steps):
        tile = jnp.minimum(t + offset[0], tiles - 1)
        for v in range(variables):
            for b, places in enumerate(where):
                source, row = places[v]
                blocks = [near[source][s, row, tile] for s in range(parts)]
                for i in range(per):
                    row = blocks[0] if i == 0 else pltpu.roll(blocks[0], (-i * levels) % LANE, 1)
                    for s in range(1, parts):
                        moved = blocks[s] if s == i else pltpu.roll(blocks[s], ((s - i) * levels) % LANE, 1)
                        row = jnp.where(lane >= s * levels, moved, row)
                    some = pl.ds(b * short, short)
                    cells[v, t * per + i, some] = state[v, t * per + i, some] + (0.05 * strength[t * per + i]) * row
        planes = pl.ds(t * per, per)
        copies.append(pltpu.make_async_copy(cells.at[:, planes], out_ref.at[:, planes], sems.at[t]))
        copies[-1].start()
    for copy in copies:
        copy.wait()


def force(state, targets, where, strength, offset, levels, planes):
    variables, nx, nz, ny = state.shape
    per = LANE // levels
    steps = -(-min(planes, nx) // per)
    owners = len(targets)
    vmem = pl.BlockSpec(memory_space=pltpu.VMEM)
    return pl.pallas_call(
        functools.partial(force_kernel, steps, per, levels, where), name="force",
        out_shape=jax.ShapeDtypeStruct(state.shape, F32),
        in_specs=[SCALARS, SCALARS] + [vmem] * (owners + 1), out_specs=pl.BlockSpec(memory_space=pl.ANY),
        scratch_shapes=[pltpu.VMEM((variables, steps * per, nz, ny), F32), pltpu.SemaphoreType.DMA((steps + 1,))],
        compiler_params=pltpu.CompilerParams(vmem_limit_bytes=16 * 2**20),
    )(offset, strength, *targets, state)


GX = ("gh", "gl")


def local(state, coeff, feed_plane):
    high, low, parts = lax.axis_size("gh"), lax.axis_size("gl"), lax.axis_size("gz")
    gx = high * low
    me = lax.axis_index("gh") * low + lax.axis_index("gl")
    variables, nx, nz, ny = state.shape
    _, modes_x, _, levels, modes = coeff.shape
    planes = feed_plane.shape[0]

    per = LANE // levels
    rows = -(-planes // per) * per
    base = jnp.reshape(me * modes_x, (1,))
    ring = [(i, (i + 1) % parts) for i in range(parts)]
    line = [(i, i + 1) for i in range(gx - 1)]
    table = span_tables(modes, nz * parts)
    edges = jnp.stack([me == 0, me == gx - 1]).astype(jnp.int32)
    plane = me * nx + jnp.arange(nx, dtype=jnp.int32)
    strength = jnp.where(plane < planes, 2.0 * jnp.square(1.0 - plane.astype(F32) / planes), 0.0)

    def spread(part):
        part = part.reshape(-1, *part.shape[2:])
        part = lax.all_to_all(part, ("gl", "gz"), split_axis=0, concat_axis=0, tiled=True)
        return part.reshape(low, parts, *part.shape[1:]).sum(0)

    relay = low == 4 and high > 1 and high & (high - 1) == 0 and variables % 2 == 0
    half = variables // 2

    def gather(part):
        stride = 1
        while stride < (high // 2 if relay else high):
            hops = [(i, i - stride) for i in range(stride, high, 2 * stride)]
            part = part + lax.ppermute(part, "gh", hops)
            stride *= 2
        if not relay:
            return part
        top = stride * low
        upper = lax.axis_index("gh") == stride
        main = lax.ppermute(part, GX, [(top + i, i) for i in range(3)])
        left = lax.ppermute(jnp.where(upper, part[:, half:], part[:, :half]), GX, [(3, 1), (top + 3, 2)])
        right = lax.ppermute(jnp.where(upper, part[:, :half], part[:, half:]), GX, [(3, 2), (top + 3, 1)])
        return part + main, left + right

    part = feed(coeff, base, feed_plane, rows, 2 * modes_x * gx, table, 0, variables, low, parts, 64, 3)
    part, edges, late = lax.optimization_barrier((part, edges, state))
    slabs = [late[:, nx - 3 :], late[:, :3]] + [jnp.stack([late[:, :, k + j] for j in range(3)]) for k in (nz - 3, 0)]
    part = spread(part)
    zlo = lax.ppermute(slabs[2], "gz", ring)
    zhi = lax.ppermute(slabs[3], "gz", [(j, i) for i, j in ring])
    acc = wall_sweep(state, edges)
    part, acc, zlo, zhi, *slabs = lax.optimization_barrier((part, acc, zlo, zhi, *slabs[:2]))
    xlo = lax.ppermute(slabs[0], GX, line)
    xhi = lax.ppermute(slabs[1], GX, [(j, i) for i, j in line])
    part = gather(part)
    span = span_sweep(state, zlo, zhi)
    part, span = lax.optimization_barrier((part, span))
    if relay:
        part, extra = part
        owned = [part] + [lax.ppermute(t, GX, [(i, 0)]) for t in (part, extra) for i in (1, 2)]
    else:
        owned = [part] + [lax.ppermute(part, GX, [(i, 0)]) for i in range(1, low)]
    new = stream_sweep(state, xlo, xhi, acc, span, edges, strength)
    for other in range(1, -(-planes // nx)):
        owned = [jnp.where(me == other, lax.ppermute(t, GX, [(0, other)]), t) for t in owned]
    offset = jnp.reshape(me * nx // per, (1,))
    where = [[(b, v) for v in range(variables)] for b in range(low)]
    if relay:
        where[3] = [(3 + v // half, v % half) for v in range(variables)]
    return force(new, owned, where, strength, offset, levels, planes)


def solution(mesh):
    gx, gz = mesh.devices.shape
    low = next(n for n in (4, 2, 1) if gx % n == 0)
    split = Mesh(mesh.devices.reshape(gx // low, low, gz), ("gh", "gl", "gz"))
    cells = P(None, GX, "gz", None)
    return jax.shard_map(
        local, mesh=split, in_specs=(cells, P(None, GX, None, "gz", None), P()), out_specs=cells, check_vma=False
    )
```
